32 devices in a mesh: row: 4 (over z), col: 4 (over x, core), rhs: 2 (over y).
Axes of the slice: x: 2, y: 2, z: 4, core: 2. Of those that a mesh axis runs over, the one named last changes fastest.
Arguments:
- lower: float32 [6, 2048, 4, 2048], P(None, 'row', None, 'col'), may hold values from -0.0625 to 0.0625
- inverse: float32 [4, 2048, 2048], P(None, ('col', 'rhs'), 'row'), may hold values from -0.125 to 0.125
- right_side: float32 [6, 2048, 2048], P(None, 'row', 'rhs'), may hold values from -6 to 6
Outputs:
- solved: float32 [4, 2048, 2048], P(None, 'col', 'rhs')
- trailing: float32 [2, 2048, 2048], P(None, 'row', 'rhs')
The draws below stay inside these ranges and needn't reach their ends.
All inputs are finite; a program needn't handle non-finite values.
Results may differ from the reference program's by a relative error of at most 0.0001.
Values sent between devices are 32-bit elements; how exact they have to be, the bound alone decides.
A program may use at most 128 MiB of HBM per device.

```python
import jax
import jax.numpy as jnp
from jax import lax

NB = 2048
NRHS = 2048
KB = 4
BLOCKS = 6


def block_levels(own_key, dims, pieces, least, largest):
    loudness, own = 1.0, jax.random.fold_in(own_key, 6)
    for axis_at, parts in pieces:
        draws = jnp.exp(jax.random.uniform(jax.random.fold_in(own, axis_at), (parts,), jnp.float32, least / len(pieces), largest / len(pieces)))
        loudness = loudness * jnp.repeat(draws, dims[axis_at] // parts).reshape([-1 if axis == axis_at else 1 for axis in range(len(dims))])
    return loudness


def bell_draw(rng, dims, scale, bound, shards=(), dtype=jnp.bfloat16):
    entries = jax.random.normal(rng, dims, jnp.float32) * scale
    if len(shards) > 0:
        entries = block_levels(rng, dims, shards, -0.22, 0.18) * entries
    return jnp.clip(entries, min=-bound, max=bound).astype(dtype)


def setup_inputs(seed: int = 0) -> dict:
    key_list = jax.random.split(jax.random.key(seed), 4)
    lower = bell_draw(key_list[0], (BLOCKS, NB, KB, NB), (KB * NB) ** -0.5, 0.0625, ((1, 4), (3, 4)), jnp.float32)
    inverse = bell_draw(key_list[1], (KB, NB, NB), NB ** -0.5, 0.125, ((1, 8), (2, 4)), jnp.float32)
    right_side = bell_draw(key_list[2], (BLOCKS, NB, NRHS), 1.0, 6.0, ((1, 4), (2, 2)), jnp.float32)
    return dict(lower=lower, inverse=inverse, right_side=right_side)


def reference(lower, inverse, right_side):
    accum = jnp.zeros_like(right_side)
    solved_list = []
    for k in range(KB):
        residual_block = right_side[k] - accum[k]
        unknowns = jnp.dot(inverse[k], residual_block, precision=lax.Precision.HIGHEST, preferred_element_type=jnp.float32)
        solved_list.append(unknowns)
        update = jnp.einsum("inc,cr->inr", lower[k + 1:, :, k, :], unknowns, precision=lax.Precision.HIGHEST)
        accum = jnp.concatenate([accum[:k + 1], accum[k + 1:] + update], axis=0)
    return jnp.stack(solved_list), right_side[KB:] - accum[KB:]
```

```python
import functools

import jax
import jax.numpy as jnp
from jax import lax
from jax.experimental import pallas as pl
from jax.experimental.pallas import tpu as pltpu
from jax.sharding import PartitionSpec as P

MESH = pl.DeviceIdType.MESH
LANES = 128


def split(value):
    high = value.astype(jnp.bfloat16)
    return high, (value - high.astype(jnp.float32)).astype(jnp.bfloat16)


def line_role(place, count):
    half = count // 2
    left = place < half
    inward = jnp.where(left, place + 1, place - 1)
    outward = jnp.where(left, place - 1, place + 1)
    from_end = jnp.where(left, place, count - 1 - place)
    return inward, outward, from_end, half - 1 - from_end


def kernel(
    dims, lower, inverse, right, solved, trailing,
    low_hi, low_lo, inv_hi, inv_lo, stage, inv_land, first, acc, zval, zin, zmid, x1, x2, x3, xin, pair,
    stage_sem, first_sem, acc_sem, inv_own_sem, inv_send, inv_recv,
    zin_recv, zmid_recv, z_in_send, z_out_send, sol_sem,
    x1_send, x1_recv, xin_recv, x2_recv, x_in_send, x_out_send, x3_send, x3_recv, tra_sem,
):
    rows_n, cols_n, rhs_n, chain, blocks, chunks, width = dims
    line_n = cols_n // 2
    zhalf, xhalf = rows_n // 2, line_n // 2
    mr, mc = acc.shape[2], zval.shape[1]
    mrh, mch = mr // 2, mc // 2
    lane_tiles = mc // LANES
    ways = lane_tiles * chain
    solved_at = rows_n - 1
    x_at = solved_at + 2
    last_at = x_at + line_n
    spacing = max(chunks, last_at + 1)
    slots = (chain - 1) * spacing + chunks + last_at

    me_row, me_col, me_rhs = lax.axis_index("row"), lax.axis_index("col"), lax.axis_index("rhs")
    core, chip = lax.rem(me_col, 2), lax.div(me_col, 2)
    sibling = me_col + 1 - 2 * core
    z_in, z_out, z_end, z_mid = line_role(me_row, rows_n)
    xc_in, xc_out, x_end, x_mid = line_role(chip, line_n)
    x_in, x_out = xc_in * 2 + core, xc_out * 2 + core
    own = pl.ds(pl.multiple_of(core * mrh, mrh), mrh)
    other = pl.ds(pl.multiple_of((1 - core) * mrh, mrh), mrh)

    barrier = pltpu.get_barrier_semaphore()

    def greet(device):
        pl.semaphore_signal(barrier, inc=1, device_id=device, device_id_type=MESH)

    greet({"row": z_in})
    greet({"col": sibling})
    greet({"col": x_in})
    for step in range(1, rhs_n):
        greet({"rhs": lax.rem(me_rhs + step, rhs_n)})
    if zhalf > 1:
        @pl.when(z_end > 0)
        def _():
            greet({"row": z_out})
    if xhalf > 1:
        @pl.when(x_end > 0)
        def _():
            greet({"col": x_out})
    count = 2 + rhs_n
    if zhalf > 1:
        count += (z_end > 0).astype(jnp.int32)
    if xhalf > 1:
        count += (x_end > 0).astype(jnp.int32)
    pl.semaphore_wait(barrier, count)

    def remote(src, dst, send, recv, device):
        return pltpu.make_async_remote_copy(
            src_ref=src, dst_ref=dst, send_sem=send, recv_sem=recv, device_id=device, device_id_type=MESH
        )

    part = inverse.shape[1]
    mine = pl.ds(pl.multiple_of(me_rhs * part, part), part)

    def inv_copy(k, step):
        return remote(
            inverse.at[k], inv_land.at[k, mine], inv_send.at[k, step - 1], inv_recv.at[k, step - 1],
            {"rhs": lax.rem(me_rhs + step, rhs_n)},
        )

    def inv_own(k):
        return pltpu.make_async_copy(inverse.at[k], inv_land.at[k, mine], inv_own_sem.at[k])

    for k in range(chain):
        for step in range(1, rhs_n):
            inv_copy(k, step).start()
        inv_own(k).start()

    def columns(c):
        return pl.ds(pl.multiple_of(c * width, width), width)

    def first_copy(c):
        return pltpu.make_async_copy(right.at[0, :, columns(c)], first.at[c], first_sem.at[c])

    def acc_copy(j, c):
        return pltpu.make_async_copy(right.at[j + 1, :, columns(c)], acc.at[j, c], acc_sem.at[j, c])

    def each_acc(action):
        @pl.loop(0, (blocks - 1) * chunks)
        def _(n):
            action(lax.div(n, chunks), lax.rem(n, chunks))

    @pl.loop(0, chunks)
    def _(c):
        first_copy(c).start()

    def stage_copy(n):
        i, half = 1 + lax.div(n, 2), lax.rem(n, 2)
        rows = pl.ds(pl.multiple_of(half * (mrh * ways), mrh * ways), mrh * ways)
        return pltpu.make_async_copy(lower.at[i, rows, :], stage.at[half], stage_sem.at[half])

    stage_copy(0).start()
    stage_copy(1).start()

    @pl.when(me_col == 0)
    def _():
        each_acc(lambda j, c: acc_copy(j, c).start())

    @pl.when(me_col != 0)
    def _():
        def clear(j, c):
            acc[j, c] = jnp.zeros((mr, width), jnp.float32)

        each_acc(clear)

    def place(k, i):
        return k * (blocks - 1) - lax.div(k * (k - 1), 2) + i - k - 1

    @pl.loop(0, 2 * (blocks - 1))
    def _(n):
        i, half = 1 + lax.div(n, 2), lax.rem(n, 2)
        rows = pl.ds(pl.multiple_of(half * mrh, mrh), mrh)
        stage_copy(n).wait()
        for k in range(chain):
            @pl.when(i > k)
            def _():
                spot = k * (blocks - 1) - (k * (k - 1)) // 2 + i - k - 1
                for tile in range(lane_tiles):
                    high, low = split(stage[half, pl.ds(tile * chain + k, mrh, stride=ways), :])
                    low_hi[spot, rows, pl.ds(tile * LANES, LANES)] = high
                    low_lo[spot, rows, pl.ds(tile * LANES, LANES)] = low

        @pl.when(n + 2 < 2 * (blocks - 1))
        def _():
            stage_copy(n + 2).start()

    @pl.loop(0, chunks)
    def _(c):
        first_copy(c).wait()

    @pl.when(me_col == 0)
    def _():
        each_acc(lambda j, c: acc_copy(j, c).wait())

    def product(high, low, depth):
        both = jnp.dot(high, pair[:depth, :], preferred_element_type=jnp.float32)
        rest = jnp.dot(low, pair[:depth, :width], preferred_element_type=jnp.float32)
        return both[:, :width] + (both[:, width:] + rest)

    def set_pair(rows, value):
        high, low = split(value)
        pair[rows, :width] = high
        pair[rows, width:] = low

    def z_rows(h):
        return pl.ds(h * mch, mch)

    def z_to_middle(k, c, h):
        return remote(zval.at[c, z_rows(h)], zmid.at[lax.rem(k, 2), c, z_rows(h)], z_in_send.at[c, h],
                      zmid_recv.at[lax.rem(k, 2), c, h], {"row": z_in})

    def z_inward(c, h):
        return remote(zval.at[c, z_rows(h)], zin.at[c, z_rows(h)], z_in_send.at[c, h], zin_recv.at[c, h], {"row": z_in})

    def z_outward(k, c, h):
        at = zmid.at[lax.rem(k, 2), c, z_rows(h)]
        return remote(at, at, z_out_send.at[c, h], zmid_recv.at[lax.rem(k, 2), c, h], {"row": z_out})

    def tail(j):
        return jnp.maximum(j - (chain - 1), 0)

    def x_first(j, c):
        return remote(acc.at[j, c, other], x1.at[tail(j), c], x1_send.at[j, c], x1_recv.at[j, c], {"col": sibling})

    def x_to_middle(j, c):
        return remote(acc.at[j, c, own], x2.at[j, c], x_in_send.at[j, c], x2_recv.at[j, c], {"col": x_in})

    def x_inward(j, c):
        return remote(acc.at[j, c, own], xin.at[j, c], x_in_send.at[j, c], xin_recv.at[j, c], {"col": x_in})

    def x_outward(j, c):
        return remote(x2.at[j, c], x2.at[j, c], x_out_send.at[j, c], x2_recv.at[j, c], {"col": x_out})

    def x_back(j, c):
        return remote(x2.at[j, c], x3.at[tail(j), c], x3_send.at[j, c], x3_recv.at[j, c], {"col": sibling})

    def solved_copy(k, c):
        return pltpu.make_async_copy(zmid.at[lax.rem(k, 2), c], solved.at[k, :, columns(c)], sol_sem.at[c])

    def trailing_own(j, c):
        return pltpu.make_async_copy(
            x2.at[j, c], trailing.at[j - (chain - 1), own, columns(c)], tra_sem.at[0, j - (chain - 1), c])

    def trailing_other(j, c):
        return pltpu.make_async_copy(
            x3.at[tail(j), c], trailing.at[j - (chain - 1), other, columns(c)], tra_sem.at[1, j - (chain - 1), c])

    def item(t, lag, then):
        u = t - lag
        n = jnp.maximum(u, 0)
        k, c = lax.div(n, spacing), lax.rem(n, spacing)

        @pl.when((u >= 0) & (k < chain) & (c < chunks))
        def _():
            then(k, c)

    def each_sum(k, action):
        stop = jnp.where(k == chain - 1, blocks - 1, k + 1)

        @pl.loop(k, stop)
        def _(j):
            action(j)

    def z_part(t, h):
        def inward_part(k, c):
            if zhalf > 1:
                @pl.when(z_end > 0)
                def _():
                    z_inward(c, h).wait_recv()
                    zval[c, z_rows(h)] += zin[c, z_rows(h)]

                @pl.when(z_mid > 0)
                def _():
                    z_inward(c, h).start()

            @pl.when(z_mid == 0)
            def _():
                z_to_middle(k, c, h).start()

        def outward_part(k, c):
            z_to_middle(k, c, h).wait_recv()

            @pl.when(z_mid == 0)
            def _():
                zmid[lax.rem(k, 2), c, z_rows(h)] += zval[c, z_rows(h)]

            if zhalf > 1:
                @pl.when(z_end > 0)
                def _():
                    z_outward(k, c, h).start()

        item(t, z_end, inward_part)
        item(t, zhalf + z_mid, outward_part)

    def x_part(t):
        def inward_part(k, c):
            def one(j):
                x_first(j, c).wait_recv()
                acc[j, c, own] += x1[tail(j), c]
                if xhalf > 1:
                    @pl.when(x_end > 0)
                    def _():
                        x_inward(j, c).wait_recv()
                        acc[j, c, own] += xin[j, c]

                    @pl.when(x_mid > 0)
                    def _():
                        x_inward(j, c).start()

                @pl.when(x_mid == 0)
                def _():
                    x_to_middle(j, c).start()

            each_sum(k, one)

        def outward_part(k, c):
            def one(j):
                x_to_middle(j, c).wait_recv()

                @pl.when(x_mid == 0)
                def _():
                    x2[j, c] += acc[j, c, own]

                x_back(j, c).start()
                if xhalf > 1:
                    @pl.when(x_end > 0)
                    def _():
                        x_outward(j, c).start()

            each_sum(k, one)

        def last_part(k, c):
            def one(j):
                x_back(j, c).wait_recv()
                x_first(j, c).wait_send()
                x_to_middle(j, c).wait_send()
                x_back(j, c).wait_send()
                if xhalf > 1:
                    @pl.when(x_end > 0)
                    def _():
                        x_outward(j, c).wait_send()

                @pl.when(k == chain - 1)
                def _():
                    trailing_own(j, c).start()
                    trailing_other(j, c).start()

            each_sum(k, one)

        item(t, x_at + x_end, inward_part)
        item(t, x_at + xhalf + x_mid, outward_part)
        item(t, last_at, last_part)

    def value_part(k, c):
        @pl.when(c == 0)
        def _():
            for step in range(1, rhs_n):
                inv_copy(k, step).wait()
            inv_own(k).wait()
            inv_hi[k], inv_lo[k] = split(inv_land[k])

        @pl.when(k == 0)
        def _():
            set_pair(pl.ds(0, mr), first[c])

        @pl.when(k > 0)
        def _():
            before = jnp.maximum(k - 1, 0)
            set_pair(own, x2[before, c])
            set_pair(other, x3[0, c])

        zval[c] = product(inv_hi[k], inv_lo[k], mr)

    def update_part(k, c):
        solved_copy(k, c).start()
        for h in range(2):
            z_inward(c, h).wait_send()
        set_pair(pl.ds(0, mc), zmid[lax.rem(k, 2), c])

        @pl.loop(k + 1, blocks)
        def _(i):
            spot = place(k, i)
            acc[i - 1, c] -= product(low_hi[spot], low_lo[spot], mc)

            @pl.when((i == k + 1) | (k == chain - 1))
            def _():
                x_first(i - 1, c).start()

    def release_part(k, c):
        solved_copy(k, c).wait()
        if zhalf > 1:
            @pl.when(z_end > 0)
            def _():
                for h in range(2):
                    z_outward(k, c, h).wait_send()

    @pl.loop(0, slots + 1)
    def _(n):
        t = n - 1
        z_part(t, 0)
        x_part(t)
        item(t, -1, value_part)
        z_part(t, 1)
        item(t, solved_at + 1, release_part)
        item(t, solved_at, update_part)

    @pl.loop(0, (blocks - chain) * chunks)
    def _(n):
        j, c = chain - 1 + lax.div(n, chunks), lax.rem(n, chunks)
        trailing_own(j, c).wait()
        trailing_other(j, c).wait()


def on_device(mesh, lower, inverse, right):
    rows_n, cols_n, rhs_n = mesh.shape["row"], mesh.shape["col"], mesh.shape["rhs"]
    blocks, mr, chain, mc = lower.shape
    width = LANES
    chunks = right.shape[2] // width
    part = inverse.shape[1]
    lane_tiles = mc // LANES
    flat = lower.reshape(blocks, mr, chain, lane_tiles, LANES).transpose(0, 1, 3, 2, 4)
    flat = flat.reshape(blocks, mr * lane_tiles * chain, LANES)
    pairs = sum(blocks - 1 - k for k in range(chain))
    sums = blocks - 1
    tails = blocks - chain
    mrh = mr // 2
    f32, bf16 = jnp.float32, jnp.bfloat16
    far = sums if cols_n > 4 else 1
    far_chunks = chunks if cols_n > 4 else 1
    dma = pltpu.SemaphoreType.DMA
    scratch = [
        pltpu.VMEM((pairs, mr, mc), bf16),
        pltpu.VMEM((pairs, mr, mc), bf16),
        pltpu.VMEM((chain, mc, mr), bf16),
        pltpu.VMEM((chain, mc, mr), bf16),
        pltpu.VMEM((2, mrh * lane_tiles * chain, LANES), f32),
        pltpu.VMEM((chain, mc, mr), f32),
        pltpu.VMEM((chunks, mr, width), f32),
        pltpu.VMEM((sums, chunks, mr, width), f32),
        pltpu.VMEM((chunks, mc, width), f32),
        pltpu.VMEM((chunks, mc, width), f32),
        pltpu.VMEM((2, chunks, mc, width), f32),
        pltpu.VMEM((tails, chunks, mrh, width), f32),
        pltpu.VMEM((sums, chunks, mrh, width), f32),
        pltpu.VMEM((tails, chunks, mrh, width), f32),
        pltpu.VMEM((far, far_chunks, mrh, width), f32),
        pltpu.VMEM((max(mr, mc), 2 * width), bf16),
        dma((2,)),
        dma((chunks,)),
        dma((sums, chunks)),
        dma((chain,)),
        dma((chain, rhs_n - 1)),
        dma((chain, rhs_n - 1)),
        dma((chunks, 2)),
        dma((2, chunks, 2)),
        dma((chunks, 2)),
        dma((chunks, 2)),
        dma((chunks,)),
        dma((sums, chunks)),
        dma((sums, chunks)),
        dma((far, far_chunks)),
        dma((sums, chunks)),
        dma((sums, chunks)),
        dma((sums, chunks)),
        dma((sums, chunks)),
        dma((sums, chunks)),
        dma((2, tails, chunks)),
    ]
    dims = (rows_n, cols_n, rhs_n, chain, blocks, chunks, width)
    any_spec = pl.BlockSpec(memory_space=pl.ANY)
    return pl.pallas_call(
        functools.partial(kernel, dims),
        out_shape=(
            jax.ShapeDtypeStruct((chain, mc, right.shape[2]), f32),
            jax.ShapeDtypeStruct((tails, mr, right.shape[2]), f32),
        ),
        in_specs=[any_spec] * 3,
        out_specs=(any_spec, any_spec),
        scratch_shapes=scratch,
        compiler_params=pltpu.CompilerParams(
            collective_id=0, has_side_effects=True, vmem_limit_bytes=62 * 1024 * 1024
        ),
        cost_estimate=pl.CostEstimate(
            flops=6 * (pairs + chain) * mr * mc * right.shape[2], bytes_accessed=4 * lower.size * 2, transcendentals=0
        ),
    )(flat, inverse, right)


def solution(mesh):
    placed = (P(None, "row", None, "col"), P(None, ("col", "rhs"), "row"), P(None, "row", "rhs"))
    return jax.shard_map(
        functools.partial(on_device, mesh),
        mesh=mesh,
        in_specs=placed,
        out_specs=(P(None, "col", "rhs"), P(None, "row", "rhs")),
        check_vma=False,
    )
```

```python
import functools

import jax
import jax.numpy as jnp
from jax import lax
from jax.experimental import pallas as pl
from jax.experimental.pallas import tpu as pltpu
from jax.sharding import PartitionSpec as P

MESH = pl.DeviceIdType.MESH
LANES = 128


def split(value):
    high = value.astype(jnp.bfloat16)
    return high, (value - high.astype(jnp.float32)).astype(jnp.bfloat16)


def line_role(place, count):
    half = count // 2
    left = place < half
    inward = jnp.where(left, place + 1, place - 1)
    outward = jnp.where(left, place - 1, place + 1)
    from_end = jnp.where(left, place, count - 1 - place)
    return inward, outward, from_end, half - 1 - from_end


def kernel(
    dims, lower, inverse, right, solved, trailing,
    low_hi, low_lo, inv_hi, inv_lo, stage, inv_land, first, acc, zval, zin, zmid, x1, x2, x3, xin, pair,
    stage_sem, first_sem, acc_sem, inv_own_sem, inv_send, inv_recv,
    zin_recv, zmid_recv, z_in_send, z_out_send, sol_sem,
    x1_send, x1_recv, xin_recv, x2_recv, x_in_send, x_out_send, x3_send, x3_recv, tra_sem,
):
    rows_n, cols_n, rhs_n, chain, blocks, chunks, width = dims
    line_n = cols_n // 2
    zhalf, xhalf = rows_n // 2, line_n // 2
    mr, mc = acc.shape[2], zval.shape[1]
    mrh, mch = mr // 2, mc // 2
    lane_tiles = mc // LANES
    ways = lane_tiles * chain
    solved_at = rows_n - 1
    x_at = solved_at + 2
    last_at = x_at + line_n
    spacing = max(chunks, last_at + 1)
    slots = (chain - 1) * spacing + chunks + last_at

    me_row, me_col, me_rhs = lax.axis_index("row"), lax.axis_index("col"), lax.axis_index("rhs")
    core, chip = lax.rem(me_col, 2), lax.div(me_col, 2)
    sibling = me_col + 1 - 2 * core
    z_in, z_out, z_end, z_mid = line_role(me_row, rows_n)
    xc_in, xc_out, x_end, x_mid = line_role(chip, line_n)
    x_in, x_out = xc_in * 2 + core, xc_out * 2 + core
    own = pl.ds(pl.multiple_of(core * mrh, mrh), mrh)
    other = pl.ds(pl.multiple_of((1 - core) * mrh, mrh), mrh)

    barrier = pltpu.get_barrier_semaphore()

    def greet(device):
        pl.semaphore_signal(barrier, inc=1, device_id=device, device_id_type=MESH)

    greet({"row": z_in})
    greet({"col": sibling})
    greet({"col": x_in})
    for step in range(1, rhs_n):
        greet({"rhs": lax.rem(me_rhs + step, rhs_n)})
    if zhalf > 1:
        @pl.when(z_end > 0)
        def _():
            greet({"row": z_out})
    if xhalf > 1:
        @pl.when(x_end > 0)
        def _():
            greet({"col": x_out})
    count = 2 + rhs_n
    if zhalf > 1:
        count += (z_end > 0).astype(jnp.int32)
    if xhalf > 1:
        count += (x_end > 0).astype(jnp.int32)
    pl.semaphore_wait(barrier, count)

    def remote(src, dst, send, recv, device):
        return pltpu.make_async_remote_copy(
            src_ref=src, dst_ref=dst, send_sem=send, recv_sem=recv, device_id=device, device_id_type=MESH
        )

    part = inverse.shape[1]
    mine = pl.ds(pl.multiple_of(me_rhs * part, part), part)

    def inv_copy(k, step):
        return remote(
            inverse.at[k], inv_land.at[k, mine], inv_send.at[k, step - 1], inv_recv.at[k, step - 1],
            {"rhs": lax.rem(me_rhs + step, rhs_n)},
        )

    def inv_own(k):
        return pltpu.make_async_copy(inverse.at[k], inv_land.at[k, mine], inv_own_sem.at[k])

    def inv_start(k):
        for step in range(1, rhs_n):
            inv_copy(k, step).start()
        inv_own(k).start()

    inv_start(0)

    def columns(c):
        return pl.ds(pl.multiple_of(c * width, width), width)

    def first_copy(c):
        return pltpu.make_async_copy(right.at[0, :, columns(c)], first.at[c], first_sem.at[c])

    def acc_copy(j, c):
        return pltpu.make_async_copy(right.at[j + 1, :, columns(c)], acc.at[j, c], acc_sem.at[j, c])

    def each_acc(action):
        @pl.loop(0, (blocks - 1) * chunks)
        def _(n):
            action(lax.div(n, chunks), lax.rem(n, chunks))

    @pl.loop(0, chunks)
    def _(c):
        first_copy(c).start()

    def stage_copy(n):
        i, half = 1 + lax.div(n, 2), lax.rem(n, 2)
        rows = pl.ds(pl.multiple_of(half * (mrh * ways), mrh * ways), mrh * ways)
        return pltpu.make_async_copy(lower.at[i, rows, :], stage.at[half], stage_sem.at[half])

    stage_copy(0).start()
    stage_copy(1).start()

    @pl.when(me_col == 0)
    def _():
        each_acc(lambda j, c: acc_copy(j, c).start())

    @pl.when(me_col != 0)
    def _():
        def clear(j, c):
            acc[j, c] = jnp.zeros((mr, width), jnp.float32)

        each_acc(clear)

    def place(k, i):
        return k * (blocks - 1) - lax.div(k * (k - 1), 2) + i - k - 1

    @pl.loop(0, 2 * (blocks - 1))
    def _(n):
        i, half = 1 + lax.div(n, 2), lax.rem(n, 2)
        rows = pl.ds(pl.multiple_of(half * mrh, mrh), mrh)
        stage_copy(n).wait()
        for k in range(chain):
            @pl.when(i > k)
            def _():
                spot = k * (blocks - 1) - (k * (k - 1)) // 2 + i - k - 1
                for tile in range(lane_tiles):
                    high, low = split(stage[half, pl.ds(tile * chain + k, mrh, stride=ways), :])
                    low_hi[spot, rows, pl.ds(tile * LANES, LANES)] = high
                    low_lo[spot, rows, pl.ds(tile * LANES, LANES)] = low

        @pl.when(n + 2 < 2 * (blocks - 1))
        def _():
            stage_copy(n + 2).start()

    @pl.loop(0, chunks)
    def _(c):
        first_copy(c).wait()

    @pl.when(me_col == 0)
    def _():
        each_acc(lambda j, c: acc_copy(j, c).wait())

    def product(high, low, depth):
        both = jnp.dot(high, pair[:depth, :], preferred_element_type=jnp.float32)
        rest = jnp.dot(low, pair[:depth, :width], preferred_element_type=jnp.float32)
        return both[:, :width] + (both[:, width:] + rest)

    def set_pair(rows, value):
        high, low = split(value)
        pair[rows, :width] = high
        pair[rows, width:] = low

    def z_rows(h):
        return pl.ds(h * mch, mch)

    def z_to_middle(k, c, h):
        return remote(zval.at[c, z_rows(h)], zmid.at[lax.rem(k, 2), c, z_rows(h)], z_in_send.at[c, h],
                      zmid_recv.at[lax.rem(k, 2), c, h], {"row": z_in})

    def z_inward(c, h):
        return remote(zval.at[c, z_rows(h)], zin.at[c, z_rows(h)], z_in_send.at[c, h], zin_recv.at[c, h], {"row": z_in})

    def z_outward(k, c, h):
        at = zmid.at[lax.rem(k, 2), c, z_rows(h)]
        return remote(at, at, z_out_send.at[c, h], zmid_recv.at[lax.rem(k, 2), c, h], {"row": z_out})

    def tail(j):
        return jnp.maximum(j - (chain - 1), 0)

    def x_first(j, c):
        return remote(acc.at[j, c, other], x1.at[tail(j), c], x1_send.at[j, c], x1_recv.at[j, c], {"col": sibling})

    def x_to_middle(j, c):
        return remote(acc.at[j, c, own], x2.at[j, c], x_in_send.at[j, c], x2_recv.at[j, c], {"col": x_in})

    def x_inward(j, c):
        return remote(acc.at[j, c, own], xin.at[j, c], x_in_send.at[j, c], xin_recv.at[j, c], {"col": x_in})

    def x_outward(j, c):
        return remote(x2.at[j, c], x2.at[j, c], x_out_send.at[j, c], x2_recv.at[j, c], {"col": x_out})

    def x_back(j, c):
        return remote(x2.at[j, c], x3.at[tail(j), c], x3_send.at[j, c], x3_recv.at[j, c], {"col": sibling})

    def solved_copy(k, c):
        return pltpu.make_async_copy(zmid.at[lax.rem(k, 2), c], solved.at[k, :, columns(c)], sol_sem.at[c])

    def trailing_own(j, c):
        return pltpu.make_async_copy(
            x2.at[j, c], trailing.at[j - (chain - 1), own, columns(c)], tra_sem.at[0, j - (chain - 1), c])

    def trailing_other(j, c):
        return pltpu.make_async_copy(
            x3.at[tail(j), c], trailing.at[j - (chain - 1), other, columns(c)], tra_sem.at[1, j - (chain - 1), c])

    def item(t, lag, then):
        u = t - lag
        n = jnp.maximum(u, 0)
        k, c = lax.div(n, spacing), lax.rem(n, spacing)

        @pl.when((u >= 0) & (k < chain) & (c < chunks))
        def _():
            then(k, c)

    def each_sum(k, action):
        stop = jnp.where(k == chain - 1, blocks - 1, k + 1)

        @pl.loop(k, stop)
        def _(j):
            action(j)

    def z_part(t, h):
        def inward_part(k, c):
            if zhalf > 1:
                @pl.when(z_end > 0)
                def _():
                    z_inward(c, h).wait_recv()
                    zval[c, z_rows(h)] += zin[c, z_rows(h)]

                @pl.when(z_mid > 0)
                def _():
                    z_inward(c, h).start()

            @pl.when(z_mid == 0)
            def _():
                z_to_middle(k, c, h).start()

        def outward_part(k, c):
            z_to_middle(k, c, h).wait_recv()

            @pl.when(z_mid == 0)
            def _():
                zmid[lax.rem(k, 2), c, z_rows(h)] += zval[c, z_rows(h)]

            if zhalf > 1:
                @pl.when(z_end > 0)
                def _():
                    z_outward(k, c, h).start()

        item(t, z_end, inward_part)
        item(t, zhalf + z_mid, outward_part)

    def x_part(t):
        def inward_part(k, c):
            def one(j):
                x_first(j, c).wait_recv()
                acc[j, c, own] += x1[tail(j), c]
                if xhalf > 1:
                    @pl.when(x_end > 0)
                    def _():
                        x_inward(j, c).wait_recv()
                        acc[j, c, own] += xin[j, c]

                    @pl.when(x_mid > 0)
                    def _():
                        x_inward(j, c).start()

                @pl.when(x_mid == 0)
                def _():
                    x_to_middle(j, c).start()

            each_sum(k, one)

        def outward_part(k, c):
            def one(j):
                x_to_middle(j, c).wait_recv()

                @pl.when(x_mid == 0)
                def _():
                    x2[j, c] += acc[j, c, own]

                x_back(j, c).start()
                if xhalf > 1:
                    @pl.when(x_end > 0)
                    def _():
                        x_outward(j, c).start()

            each_sum(k, one)

        def last_part(k, c):
            def one(j):
                x_back(j, c).wait_recv()
                x_first(j, c).wait_send()
                x_to_middle(j, c).wait_send()
                x_back(j, c).wait_send()
                if xhalf > 1:
                    @pl.when(x_end > 0)
                    def _():
                        x_outward(j, c).wait_send()

                @pl.when(k == chain - 1)
                def _():
                    trailing_own(j, c).start()
                    trailing_other(j, c).start()

            each_sum(k, one)

        item(t, x_at + x_end, inward_part)
        item(t, x_at + xhalf + x_mid, outward_part)
        item(t, last_at, last_part)

    def value_part(k, c):
        @pl.when(c == 0)
        def _():
            for step in range(1, rhs_n):
                inv_copy(k, step).wait()
            inv_own(k).wait()

            @pl.when(k + 1 < chain)
            def _():
                inv_start(k + 1)

            inv_hi[k], inv_lo[k] = split(inv_land[k])

        @pl.when(k == 0)
        def _():
            set_pair(pl.ds(0, mr), first[c])

        @pl.when(k > 0)
        def _():
            before = jnp.maximum(k - 1, 0)
            set_pair(own, x2[before, c])
            set_pair(other, x3[0, c])

        zval[c] = product(inv_hi[k], inv_lo[k], mr)

    def update_part(k, c):
        solved_copy(k, c).start()
        for h in range(2):
            z_inward(c, h).wait_send()
        set_pair(pl.ds(0, mc), zmid[lax.rem(k, 2), c])

        @pl.loop(k + 1, blocks)
        def _(i):
            spot = place(k, i)
            acc[i - 1, c] -= product(low_hi[spot], low_lo[spot], mc)

            @pl.when((i == k + 1) | (k == chain - 1))
            def _():
                x_first(i - 1, c).start()

    def release_part(k, c):
        solved_copy(k, c).wait()
        if zhalf > 1:
            @pl.when(z_end > 0)
            def _():
                for h in range(2):
                    z_outward(k, c, h).wait_send()

    @pl.loop(0, slots + 1)
    def _(n):
        t = n - 1
        z_part(t, 0)
        x_part(t)
        item(t, -1, value_part)
        z_part(t, 1)
        item(t, solved_at + 1, release_part)
        item(t, solved_at, update_part)

    @pl.loop(0, (blocks - chain) * chunks)
    def _(n):
        j, c = chain - 1 + lax.div(n, chunks), lax.rem(n, chunks)
        trailing_own(j, c).wait()
        trailing_other(j, c).wait()


def hand_over(solved, trailing, solved_out, trailing_out, solved_sem, trailing_sem):
    copies = []
    for src, dst, sems in ((solved, solved_out, solved_sem), (trailing, trailing_out, trailing_sem)):
        rows = src.shape[1] // 2
        for k in range(src.shape[0]):
            for half in range(2):
                at = pl.ds(half * rows, rows)
                copies.append(pltpu.make_async_copy(src.at[k, at], dst.at[k, at], sems.at[k, half]))
    for copy in copies:
        copy.start()
    for copy in copies:
        copy.wait()


def on_device(mesh, lower, inverse, right):
    rows_n, cols_n, rhs_n = mesh.shape["row"], mesh.shape["col"], mesh.shape["rhs"]
    blocks, mr, chain, mc = lower.shape
    width = LANES
    chunks = right.shape[2] // width
    part = inverse.shape[1]
    lane_tiles = mc // LANES
    flat = lower.reshape(blocks, mr, chain, lane_tiles, LANES).transpose(0, 1, 3, 2, 4)
    flat = flat.reshape(blocks, mr * lane_tiles * chain, LANES)
    pairs = sum(blocks - 1 - k for k in range(chain))
    sums = blocks - 1
    tails = blocks - chain
    mrh = mr // 2
    f32, bf16 = jnp.float32, jnp.bfloat16
    far = sums if cols_n > 4 else 1
    far_chunks = chunks if cols_n > 4 else 1
    dma = pltpu.SemaphoreType.DMA
    scratch = [
        pltpu.VMEM((pairs, mr, mc), bf16),
        pltpu.VMEM((pairs, mr, mc), bf16),
        pltpu.VMEM((chain, mc, mr), bf16),
        pltpu.VMEM((chain, mc, mr), bf16),
        pltpu.VMEM((2, mrh * lane_tiles * chain, LANES), f32),
        pltpu.VMEM((chain, mc, mr), f32),
        pltpu.VMEM((chunks, mr, width), f32),
        pltpu.VMEM((sums, chunks, mr, width), f32),
        pltpu.VMEM((chunks, mc, width), f32),
        pltpu.VMEM((chunks, mc, width), f32),
        pltpu.VMEM((2, chunks, mc, width), f32),
        pltpu.VMEM((tails, chunks, mrh, width), f32),
        pltpu.VMEM((sums, chunks, mrh, width), f32),
        pltpu.VMEM((tails, chunks, mrh, width), f32),
        pltpu.VMEM((far, far_chunks, mrh, width), f32),
        pltpu.VMEM((max(mr, mc), 2 * width), bf16),
        dma((2,)),
        dma((chunks,)),
        dma((sums, chunks)),
        dma((chain,)),
        dma((chain, rhs_n - 1)),
        dma((chain, rhs_n - 1)),
        dma((chunks, 2)),
        dma((2, chunks, 2)),
        dma((chunks, 2)),
        dma((chunks, 2)),
        dma((chunks,)),
        dma((sums, chunks)),
        dma((sums, chunks)),
        dma((far, far_chunks)),
        dma((sums, chunks)),
        dma((sums, chunks)),
        dma((sums, chunks)),
        dma((sums, chunks)),
        dma((sums, chunks)),
        dma((2, tails, chunks)),
    ]
    dims = (rows_n, cols_n, rhs_n, chain, blocks, chunks, width)
    any_spec = pl.BlockSpec(memory_space=pl.ANY)
    found = pl.pallas_call(
        functools.partial(kernel, dims),
        out_shape=(
            jax.ShapeDtypeStruct((chain, mc, right.shape[2]), f32),
            jax.ShapeDtypeStruct((tails, mr, right.shape[2]), f32),
        ),
        in_specs=[any_spec] * 3,
        out_specs=(any_spec, any_spec),
        scratch_shapes=scratch,
        compiler_params=pltpu.CompilerParams(
            collective_id=0, has_side_effects=True, vmem_limit_bytes=62 * 1024 * 1024
        ),
        cost_estimate=pl.CostEstimate(
            flops=6 * (pairs + chain) * mr * mc * right.shape[2], bytes_accessed=4 * lower.size * 2, transcendentals=0
        ),
    )(flat, inverse, right)
    shapes = tuple(jax.ShapeDtypeStruct(array.shape, array.dtype) for array in found)
    return pl.pallas_call(
        hand_over,
        out_shape=shapes,
        in_specs=[any_spec] * 2,
        out_specs=(any_spec, any_spec),
        scratch_shapes=[dma((chain, 2)), dma((tails, 2))],
        cost_estimate=pl.CostEstimate(
            flops=0, bytes_accessed=8 * sum(array.size for array in found), transcendentals=0
        ),
    )(*found)


def solution(mesh):
    placed = (P(None, "row", None, "col"), P(None, ("col", "rhs"), "row"), P(None, "row", "rhs"))
    return jax.shard_map(
        functools.partial(on_device, mesh),
        mesh=mesh,
        in_specs=placed,
        out_specs=(P(None, "col", "rhs"), P(None, "row", "rhs")),
        check_vma=False,
    )
```

```python
import functools

import jax
import jax.numpy as jnp
from jax import lax
from jax.experimental import pallas as pl
from jax.experimental.pallas import tpu as pltpu
from jax.sharding import PartitionSpec as P

MESH = pl.DeviceIdType.MESH
LANES = 128


def split(value):
    high = value.astype(jnp.bfloat16)
    return high, (value - high.astype(jnp.float32)).astype(jnp.bfloat16)


def line_role(place, count):
    half = count // 2
    left = place < half
    inward = jnp.where(left, place + 1, place - 1)
    outward = jnp.where(left, place - 1, place + 1)
    from_end = jnp.where(left, place, count - 1 - place)
    return inward, outward, from_end, half - 1 - from_end


def kernel(
    dims, lower, inverse, right, solved, trailing,
    low_hi, low_lo, inv_hi, inv_lo, stage, inv_land, first, acc, zval, zin, zmid, x1, x2, x3, xin, pair,
    stage_sem, first_sem, acc_sem, inv_own_sem, inv_send, inv_recv,
    zin_recv, zmid_recv, z_in_send, z_out_send, sol_sem,
    x1_send, x1_recv, xin_recv, x2_recv, x_in_send, x_out_send, x3_send, x3_recv, tra_sem,
):
    rows_n, cols_n, rhs_n, chain, blocks, chunks, width = dims
    line_n = cols_n // 2
    zhalf, xhalf = rows_n // 2, line_n // 2
    mr, mc = acc.shape[2], zval.shape[1]
    mrh, mch = mr // 2, mc // 2
    solved_at = rows_n - 1
    x_at = solved_at + 2
    last_at = x_at + line_n
    spacing = max(chunks, last_at + 1)
    slots = (chain - 1) * spacing + chunks + last_at

    me_row, me_col, me_rhs = lax.axis_index("row"), lax.axis_index("col"), lax.axis_index("rhs")
    core, chip = lax.rem(me_col, 2), lax.div(me_col, 2)
    sibling = me_col + 1 - 2 * core
    z_in, z_out, z_end, z_mid = line_role(me_row, rows_n)
    xc_in, xc_out, x_end, x_mid = line_role(chip, line_n)
    x_in, x_out = xc_in * 2 + core, xc_out * 2 + core
    own = pl.ds(pl.multiple_of(core * mrh, mrh), mrh)
    other = pl.ds(pl.multiple_of((1 - core) * mrh, mrh), mrh)

    barrier = pltpu.get_barrier_semaphore()

    def greet(device):
        pl.semaphore_signal(barrier, inc=1, device_id=device, device_id_type=MESH)

    greet({"row": z_in})
    greet({"col": sibling})
    greet({"col": x_in})
    for step in range(1, rhs_n):
        greet({"rhs": lax.rem(me_rhs + step, rhs_n)})
    if zhalf > 1:
        @pl.when(z_end > 0)
        def _():
            greet({"row": z_out})
    if xhalf > 1:
        @pl.when(x_end > 0)
        def _():
            greet({"col": x_out})
    count = 2 + rhs_n
    if zhalf > 1:
        count += (z_end > 0).astype(jnp.int32)
    if xhalf > 1:
        count += (x_end > 0).astype(jnp.int32)
    pl.semaphore_wait(barrier, count)

    def remote(src, dst, send, recv, device):
        return pltpu.make_async_remote_copy(
            src_ref=src, dst_ref=dst, send_sem=send, recv_sem=recv, device_id=device, device_id_type=MESH
        )

    part = inverse.shape[1]
    mine = pl.ds(pl.multiple_of(me_rhs * part, part), part)

    def inv_copy(k, step):
        return remote(
            inverse.at[k], inv_land.at[k, mine], inv_send.at[k, step - 1], inv_recv.at[k, step - 1],
            {"rhs": lax.rem(me_rhs + step, rhs_n)},
        )

    def inv_own(k):
        return pltpu.make_async_copy(inverse.at[k], inv_land.at[k, mine], inv_own_sem.at[k])

    def inv_start(k):
        for step in range(1, rhs_n):
            inv_copy(k, step).start()
        inv_own(k).start()

    inv_start(0)

    def columns(c):
        return pl.ds(pl.multiple_of(c * width, width), width)

    def first_copy(c):
        return pltpu.make_async_copy(right.at[0, :, columns(c)], first.at[c], first_sem.at[c])

    def acc_copy(j, c):
        return pltpu.make_async_copy(right.at[j + 1, :, columns(c)], acc.at[j, c], acc_sem.at[j, c])

    def each_acc(action):
        @pl.loop(0, (blocks - 1) * chunks)
        def _(n):
            action(lax.div(n, chunks), lax.rem(n, chunks))

    @pl.loop(0, chunks)
    def _(c):
        first_copy(c).start()

    pairs, slot_n = low_hi.shape[0], stage.shape[0]

    def place(k, i):
        return k * (blocks - 1) - lax.div(k * (k - 1), 2) + i - k - 1

    def stage_copy(spot, action):
        for k in range(chain):
            begin = k * (blocks - 1) - (k * (k - 1)) // 2
            end = begin + blocks - 1 - k

            @pl.when((spot >= begin) & (spot < end))
            def _():
                at = lax.rem(spot, slot_n)
                action(pltpu.make_async_copy(lower.at[spot - begin + k + 1, :, k, :], stage.at[at], stage_sem.at[at]))

    def take_block(spot):
        @pl.when((spot >= 0) & (spot < pairs))
        def _():
            stage_copy(spot, lambda copy: copy.wait())
            low_hi[spot], low_lo[spot] = split(stage[lax.rem(spot, slot_n)])

            @pl.when(spot + slot_n < pairs)
            def _():
                stage_copy(spot + slot_n, lambda copy: copy.start())

    @pl.loop(0, min(slot_n, pairs))
    def _(spot):
        stage_copy(spot, lambda copy: copy.start())

    @pl.when(me_col == 0)
    def _():
        each_acc(lambda j, c: acc_copy(j, c).start())

    @pl.when(me_col != 0)
    def _():
        def clear(j, c):
            acc[j, c] = jnp.zeros((mr, width), jnp.float32)

        each_acc(clear)

    take_block(0)

    @pl.loop(0, chunks)
    def _(c):
        first_copy(c).wait()

    def product(high, low, depth):
        both = jnp.dot(high, pair[:depth, :], preferred_element_type=jnp.float32)
        rest = jnp.dot(low, pair[:depth, :width], preferred_element_type=jnp.float32)
        return both[:, :width] + (both[:, width:] + rest)

    def set_pair(rows, value):
        high, low = split(value)
        pair[rows, :width] = high
        pair[rows, width:] = low

    def z_rows(h):
        return pl.ds(h * mch, mch)

    def z_to_middle(k, c, h):
        return remote(zval.at[c, z_rows(h)], zmid.at[lax.rem(k, 2), c, z_rows(h)], z_in_send.at[c, h],
                      zmid_recv.at[lax.rem(k, 2), c, h], {"row": z_in})

    def z_inward(c, h):
        return remote(zval.at[c, z_rows(h)], zin.at[c, z_rows(h)], z_in_send.at[c, h], zin_recv.at[c, h], {"row": z_in})

    def z_outward(k, c, h):
        at = zmid.at[lax.rem(k, 2), c, z_rows(h)]
        return remote(at, at, z_out_send.at[c, h], zmid_recv.at[lax.rem(k, 2), c, h], {"row": z_out})

    def tail(j):
        return jnp.maximum(j - (chain - 1), 0)

    def x_first(j, c):
        return remote(acc.at[j, c, other], x1.at[tail(j), c], x1_send.at[j, c], x1_recv.at[j, c], {"col": sibling})

    def x_to_middle(j, c):
        return remote(acc.at[j, c, own], x2.at[j, c], x_in_send.at[j, c], x2_recv.at[j, c], {"col": x_in})

    def x_inward(j, c):
        return remote(acc.at[j, c, own], xin.at[j, c], x_in_send.at[j, c], xin_recv.at[j, c], {"col": x_in})

    def x_outward(j, c):
        return remote(x2.at[j, c], x2.at[j, c], x_out_send.at[j, c], x2_recv.at[j, c], {"col": x_out})

    def x_back(j, c):
        return remote(x2.at[j, c], x3.at[tail(j), c], x3_send.at[j, c], x3_recv.at[j, c], {"col": sibling})

    def solved_copy(k, c):
        return pltpu.make_async_copy(zmid.at[lax.rem(k, 2), c], solved.at[k, :, columns(c)], sol_sem.at[c])

    def trailing_own(j, c):
        return pltpu.make_async_copy(
            x2.at[j, c], trailing.at[j - (chain - 1), own, columns(c)], tra_sem.at[0, j - (chain - 1), c])

    def trailing_other(j, c):
        return pltpu.make_async_copy(
            x3.at[tail(j), c], trailing.at[j - (chain - 1), other, columns(c)], tra_sem.at[1, j - (chain - 1), c])

    def item(t, lag, then):
        u = t - lag
        n = jnp.maximum(u, 0)
        k, c = lax.div(n, spacing), lax.rem(n, spacing)

        @pl.when((u >= 0) & (k < chain) & (c < chunks))
        def _():
            then(k, c)

    def each_sum(k, action):
        stop = jnp.where(k == chain - 1, blocks - 1, k + 1)

        @pl.loop(k, stop)
        def _(j):
            action(j)

    def z_part(t, h):
        def inward_part(k, c):
            if zhalf > 1:
                @pl.when(z_end > 0)
                def _():
                    z_inward(c, h).wait_recv()
                    zval[c, z_rows(h)] += zin[c, z_rows(h)]

                @pl.when(z_mid > 0)
                def _():
                    z_inward(c, h).start()

            @pl.when(z_mid == 0)
            def _():
                z_to_middle(k, c, h).start()

        def outward_part(k, c):
            z_to_middle(k, c, h).wait_recv()

            @pl.when(z_mid == 0)
            def _():
                zmid[lax.rem(k, 2), c, z_rows(h)] += zval[c, z_rows(h)]

            if zhalf > 1:
                @pl.when(z_end > 0)
                def _():
                    z_outward(k, c, h).start()

        item(t, z_end, inward_part)
        item(t, zhalf + z_mid, outward_part)

    def x_part(t):
        def inward_part(k, c):
            def one(j):
                x_first(j, c).wait_recv()
                acc[j, c, own] += x1[tail(j), c]
                if xhalf > 1:
                    @pl.when(x_end > 0)
                    def _():
                        x_inward(j, c).wait_recv()
                        acc[j, c, own] += xin[j, c]

                    @pl.when(x_mid > 0)
                    def _():
                        x_inward(j, c).start()

                @pl.when(x_mid == 0)
                def _():
                    x_to_middle(j, c).start()

            each_sum(k, one)

        def outward_part(k, c):
            def one(j):
                x_to_middle(j, c).wait_recv()

                @pl.when(x_mid == 0)
                def _():
                    x2[j, c] += acc[j, c, own]

                x_back(j, c).start()
                if xhalf > 1:
                    @pl.when(x_end > 0)
                    def _():
                        x_outward(j, c).start()

            each_sum(k, one)

        def last_part(k, c):
            def one(j):
                x_back(j, c).wait_recv()
                x_first(j, c).wait_send()
                x_to_middle(j, c).wait_send()
                x_back(j, c).wait_send()
                if xhalf > 1:
                    @pl.when(x_end > 0)
                    def _():
                        x_outward(j, c).wait_send()

                @pl.when(k == chain - 1)
                def _():
                    trailing_own(j, c).start()
                    trailing_other(j, c).start()

            each_sum(k, one)

        item(t, x_at + x_end, inward_part)
        item(t, x_at + xhalf + x_mid, outward_part)
        item(t, last_at, last_part)

    def value_part(k, c):
        @pl.when(c == 0)
        def _():
            for step in range(1, rhs_n):
                inv_copy(k, step).wait()
            inv_own(k).wait()

            @pl.when(k + 1 < chain)
            def _():
                inv_start(k + 1)

            inv_hi[k], inv_lo[k] = split(inv_land[k])

        @pl.when(k == 0)
        def _():
            set_pair(pl.ds(0, mr), first[c])

        @pl.when(k > 0)
        def _():
            before = jnp.maximum(k - 1, 0)
            set_pair(own, x2[before, c])
            set_pair(other, x3[0, c])

        zval[c] = product(inv_hi[k], inv_lo[k], mr)

    def update_part(k, c):
        solved_copy(k, c).start()
        for h in range(2):
            z_inward(c, h).wait_send()
        set_pair(pl.ds(0, mc), zmid[lax.rem(k, 2), c])

        @pl.loop(k + 1, blocks)
        def _(i):
            spot = place(k, i)
            acc[i - 1, c] -= product(low_hi[spot], low_lo[spot], mc)

            @pl.when((i == k + 1) | (k == chain - 1))
            def _():
                x_first(i - 1, c).start()

    def release_part(k, c):
        solved_copy(k, c).wait()
        if zhalf > 1:
            @pl.when(z_end > 0)
            def _():
                for h in range(2):
                    z_outward(k, c, h).wait_send()

    @pl.loop(0, slots + 1)
    def _(n):
        t = n - 1
        z_part(t, 0)
        x_part(t)
        item(t, -1, value_part)
        z_part(t, 1)
        item(t, solved_at + 1, release_part)

        @pl.when((t == 0) & (me_col == 0))
        def _():
            each_acc(lambda j, c: acc_copy(j, c).wait())

        item(t, solved_at, update_part)
        take_block(t + 2)

    @pl.loop(0, (blocks - chain) * chunks)
    def _(n):
        j, c = chain - 1 + lax.div(n, chunks), lax.rem(n, chunks)
        trailing_own(j, c).wait()
        trailing_other(j, c).wait()


def hand_over(solved, trailing, solved_out, trailing_out, solved_buf, trailing_buf, solved_sem, trailing_sem):
    jobs = []
    for src, buf, dst, sems in (
        (solved, solved_buf, solved_out, solved_sem), (trailing, trailing_buf, trailing_out, trailing_sem),
    ):
        rows = src.shape[1] // 2
        for k in range(src.shape[0]):
            for half in range(2):
                at = pl.ds(half * rows, rows)
                jobs.append((
                    pltpu.make_async_copy(src.at[k, at], buf.at[k, at], sems.at[0, k, half]),
                    pltpu.make_async_copy(buf.at[k, at], dst.at[k, at], sems.at[1, k, half]),
                ))
    for come, _ in jobs:
        come.start()
    for come, go in jobs:
        come.wait()
        go.start()
    for _, go in jobs:
        go.wait()


def on_device(mesh, lower, inverse, right):
    rows_n, cols_n, rhs_n = mesh.shape["row"], mesh.shape["col"], mesh.shape["rhs"]
    blocks, mr, chain, mc = lower.shape
    width = LANES
    chunks = right.shape[2] // width
    part = inverse.shape[1]
    pairs = sum(blocks - 1 - k for k in range(chain))
    sums = blocks - 1
    stages = min(4, pairs)
    tails = blocks - chain
    mrh = mr // 2
    f32, bf16 = jnp.float32, jnp.bfloat16
    far = sums if cols_n > 4 else 1
    far_chunks = chunks if cols_n > 4 else 1
    dma = pltpu.SemaphoreType.DMA
    scratch = [
        pltpu.VMEM((pairs, mr, mc), bf16),
        pltpu.VMEM((pairs, mr, mc), bf16),
        pltpu.VMEM((chain, mc, mr), bf16),
        pltpu.VMEM((chain, mc, mr), bf16),
        pltpu.VMEM((stages, mr, mc), f32),
        pltpu.VMEM((chain, mc, mr), f32),
        pltpu.VMEM((chunks, mr, width), f32),
        pltpu.VMEM((sums, chunks, mr, width), f32),
        pltpu.VMEM((chunks, mc, width), f32),
        pltpu.VMEM((chunks, mc, width), f32),
        pltpu.VMEM((2, chunks, mc, width), f32),
        pltpu.VMEM((tails, chunks, mrh, width), f32),
        pltpu.VMEM((sums, chunks, mrh, width), f32),
        pltpu.VMEM((tails, chunks, mrh, width), f32),
        pltpu.VMEM((far, far_chunks, mrh, width), f32),
        pltpu.VMEM((max(mr, mc), 2 * width), bf16),
        dma((stages,)),
        dma((chunks,)),
        dma((sums, chunks)),
        dma((chain,)),
        dma((chain, rhs_n - 1)),
        dma((chain, rhs_n - 1)),
        dma((chunks, 2)),
        dma((2, chunks, 2)),
        dma((chunks, 2)),
        dma((chunks, 2)),
        dma((chunks,)),
        dma((sums, chunks)),
        dma((sums, chunks)),
        dma((far, far_chunks)),
        dma((sums, chunks)),
        dma((sums, chunks)),
        dma((sums, chunks)),
        dma((sums, chunks)),
        dma((sums, chunks)),
        dma((2, tails, chunks)),
    ]
    dims = (rows_n, cols_n, rhs_n, chain, blocks, chunks, width)
    any_spec = pl.BlockSpec(memory_space=pl.ANY)
    found = pl.pallas_call(
        functools.partial(kernel, dims),
        out_shape=(
            jax.ShapeDtypeStruct((chain, mc, right.shape[2]), f32),
            jax.ShapeDtypeStruct((tails, mr, right.shape[2]), f32),
        ),
        in_specs=[any_spec] * 3,
        out_specs=(any_spec, any_spec),
        scratch_shapes=scratch,
        compiler_params=pltpu.CompilerParams(
            collective_id=0, has_side_effects=True, vmem_limit_bytes=62 * 1024 * 1024
        ),
        cost_estimate=pl.CostEstimate(
            flops=6 * (pairs + chain) * mr * mc * right.shape[2], bytes_accessed=4 * lower.size * 2, transcendentals=0
        ),
    )(lower, inverse, right)
    shapes = tuple(jax.ShapeDtypeStruct(array.shape, array.dtype) for array in found)
    return pl.pallas_call(
        hand_over,
        out_shape=shapes,
        in_specs=[any_spec] * 2,
        out_specs=(any_spec, any_spec),
        scratch_shapes=[
            *(pltpu.VMEM(shape.shape, shape.dtype) for shape in shapes),
            dma((2, chain, 2)),
            dma((2, tails, 2)),
        ],
        compiler_params=pltpu.CompilerParams(vmem_limit_bytes=32 * 1024 * 1024),
        cost_estimate=pl.CostEstimate(
            flops=0, bytes_accessed=8 * sum(array.size for array in found), transcendentals=0
        ),
    )(*found)


def solution(mesh):
    placed = (P(None, "row", None, "col"), P(None, ("col", "rhs"), "row"), P(None, "row", "rhs"))
    return jax.shard_map(
        functools.partial(on_device, mesh),
        mesh=mesh,
        in_specs=placed,
        out_specs=(P(None, "col", "rhs"), P(None, "row", "rhs")),
        check_vma=False,
    )
```

```python
import functools

import jax
import jax.numpy as jnp
from jax import lax
from jax.experimental import pallas as pl
from jax.experimental.pallas import tpu as pltpu
from jax.sharding import PartitionSpec as P

MESH = pl.DeviceIdType.MESH
LANES = 128


def split(value):
    high = value.astype(jnp.bfloat16)
    return high, (value - high.astype(jnp.float32)).astype(jnp.bfloat16)


def line_role(place, count):
    half = count // 2
    left = place < half
    inward = jnp.where(left, place + 1, place - 1)
    outward = jnp.where(left, place - 1, place + 1)
    from_end = jnp.where(left, place, count - 1 - place)
    return inward, outward, from_end, half - 1 - from_end


def kernel(
    dims, lower, inverse, right, solved, trailing,
    low_hi, low_lo, inv_hi, inv_lo, stage, inv_land, first, acc, zval, zin, zmid, x1, x2, x3, xin, pair, duo,
    stage_sem, first_sem, acc_sem, inv_own_sem, inv_send, inv_recv,
    zin_recv, zmid_recv, z_in_send, z_out_send, sol_sem,
    x1_send, x1_recv, xin_recv, x2_recv, x_in_send, x_out_send, x3_send, x3_recv, tra_sem,
):
    rows_n, cols_n, rhs_n, chain, blocks, chunks, width = dims
    line_n = cols_n // 2
    zhalf, xhalf = rows_n // 2, line_n // 2
    mr, mc = acc.shape[2], zval.shape[1]
    mrh, mch = mr // 2, mc // 2
    solved_at = rows_n - 1
    x_at = solved_at + 1
    last_at = x_at + line_n
    spacing = max(chunks, last_at + 1)
    slots = (chain - 1) * spacing + chunks + last_at

    me_row, me_col, me_rhs = lax.axis_index("row"), lax.axis_index("col"), lax.axis_index("rhs")
    core, chip = lax.rem(me_col, 2), lax.div(me_col, 2)
    sibling = me_col + 1 - 2 * core
    z_in, z_out, z_end, z_mid = line_role(me_row, rows_n)
    xc_in, xc_out, x_end, x_mid = line_role(chip, line_n)
    x_in, x_out = xc_in * 2 + core, xc_out * 2 + core
    own = pl.ds(pl.multiple_of(core * mrh, mrh), mrh)
    other = pl.ds(pl.multiple_of((1 - core) * mrh, mrh), mrh)

    barrier = pltpu.get_barrier_semaphore()

    def greet(device):
        pl.semaphore_signal(barrier, inc=1, device_id=device, device_id_type=MESH)

    greet({"row": z_in})
    greet({"col": sibling})
    greet({"col": x_in})
    for step in range(1, rhs_n):
        greet({"rhs": lax.rem(me_rhs + step, rhs_n)})
    if zhalf > 1:
        @pl.when(z_end > 0)
        def _():
            greet({"row": z_out})
    if xhalf > 1:
        @pl.when(x_end > 0)
        def _():
            greet({"col": x_out})
    count = 2 + rhs_n
    if zhalf > 1:
        count += (z_end > 0).astype(jnp.int32)
    if xhalf > 1:
        count += (x_end > 0).astype(jnp.int32)
    pl.semaphore_wait(barrier, count)

    def remote(src, dst, send, recv, device):
        return pltpu.make_async_remote_copy(
            src_ref=src, dst_ref=dst, send_sem=send, recv_sem=recv, device_id=device, device_id_type=MESH
        )

    part = inverse.shape[1]
    mine = pl.ds(pl.multiple_of(me_rhs * part, part), part)

    def inv_copy(k, step):
        return remote(
            inverse.at[k], inv_land.at[k, mine], inv_send.at[k, step - 1], inv_recv.at[k, step - 1],
            {"rhs": lax.rem(me_rhs + step, rhs_n)},
        )

    def inv_own(k):
        return pltpu.make_async_copy(inverse.at[k], inv_land.at[k, mine], inv_own_sem.at[k])

    def inv_start(k):
        for step in range(1, rhs_n):
            inv_copy(k, step).start()
        inv_own(k).start()

    inv_start(0)

    def columns(c):
        return pl.ds(pl.multiple_of(c * width, width), width)

    def first_copy(c):
        return pltpu.make_async_copy(right.at[0, :, columns(c)], first.at[c], first_sem.at[c])

    def acc_copy(j, c):
        return pltpu.make_async_copy(right.at[j + 1, :, columns(c)], acc.at[j, c], acc_sem.at[j, c])

    def each_acc(action):
        @pl.loop(0, (blocks - 1) * chunks)
        def _(n):
            action(lax.div(n, chunks), lax.rem(n, chunks))

    @pl.loop(0, chunks)
    def _(c):
        first_copy(c).start()

    pairs, slot_n = low_hi.shape[0], stage.shape[0]

    def place(k, i):
        return k * (blocks - 1) - lax.div(k * (k - 1), 2) + i - k - 1

    def stage_copy(spot, action):
        for k in range(chain):
            begin = k * (blocks - 1) - (k * (k - 1)) // 2
            end = begin + blocks - 1 - k

            @pl.when((spot >= begin) & (spot < end))
            def _():
                at = lax.rem(spot, slot_n)
                action(pltpu.make_async_copy(lower.at[spot - begin + k + 1, :, k, :], stage.at[at], stage_sem.at[at]))

    def take_block(spot):
        @pl.when((spot >= 0) & (spot < pairs))
        def _():
            stage_copy(spot, lambda copy: copy.wait())
            low_hi[spot], low_lo[spot] = split(stage[lax.rem(spot, slot_n)])

            @pl.when(spot + slot_n < pairs)
            def _():
                stage_copy(spot + slot_n, lambda copy: copy.start())

    @pl.loop(0, min(slot_n, pairs))
    def _(spot):
        stage_copy(spot, lambda copy: copy.start())

    @pl.when(me_col == 0)
    def _():
        each_acc(lambda j, c: acc_copy(j, c).start())

    @pl.when(me_col != 0)
    def _():
        def clear(j, c):
            acc[j, c] = jnp.zeros((mr, width), jnp.float32)

        each_acc(clear)

    take_block(0)

    @pl.loop(0, chunks)
    def _(c):
        first_copy(c).wait()

    def product(high, low, depth):
        both = jnp.dot(high, pair[:depth, :], preferred_element_type=jnp.float32)
        rest = jnp.dot(low, pair[:depth, :width], preferred_element_type=jnp.float32)
        return both[:, :width] + (both[:, width:] + rest)

    def set_pair(rows, value):
        high, low = split(value)
        pair[rows, :width] = high
        pair[rows, width:] = low

    def z_rows(h):
        return pl.ds(h * mch, mch)

    def z_to_middle(k, c, h):
        return remote(zval.at[c, z_rows(h)], zmid.at[lax.rem(k, 2), c, z_rows(h)], z_in_send.at[c, h],
                      zmid_recv.at[lax.rem(k, 2), c, h], {"row": z_in})

    def z_inward(c, h):
        return remote(zval.at[c, z_rows(h)], zin.at[c, z_rows(h)], z_in_send.at[c, h], zin_recv.at[c, h], {"row": z_in})

    def z_outward(k, c, h):
        at = zmid.at[lax.rem(k, 2), c, z_rows(h)]
        return remote(at, at, z_out_send.at[c, h], zmid_recv.at[lax.rem(k, 2), c, h], {"row": z_out})

    def tail(j):
        return jnp.maximum(j - (chain - 1), 0)

    def x_first(j, c):
        return remote(acc.at[j, c, other], x1.at[tail(j), c], x1_send.at[j, c], x1_recv.at[j, c], {"col": sibling})

    def x_to_middle(j, c):
        return remote(acc.at[j, c, own], x2.at[j, c], x_in_send.at[j, c], x2_recv.at[j, c], {"col": x_in})

    def x_inward(j, c):
        return remote(acc.at[j, c, own], xin.at[j, c], x_in_send.at[j, c], xin_recv.at[j, c], {"col": x_in})

    def x_outward(j, c):
        return remote(x2.at[j, c], x2.at[j, c], x_out_send.at[j, c], x2_recv.at[j, c], {"col": x_out})

    def x_back(j, c):
        return remote(x2.at[j, c], x3.at[tail(j), c], x3_send.at[j, c], x3_recv.at[j, c], {"col": sibling})

    def solved_copy(k, c):
        return pltpu.make_async_copy(zmid.at[lax.rem(k, 2), c], solved.at[k, :, columns(c)], sol_sem.at[c])

    def trailing_own(j, c):
        return pltpu.make_async_copy(
            x2.at[j, c], trailing.at[j - (chain - 1), own, columns(c)], tra_sem.at[0, j - (chain - 1), c])

    def trailing_other(j, c):
        return pltpu.make_async_copy(
            x3.at[tail(j), c], trailing.at[j - (chain - 1), other, columns(c)], tra_sem.at[1, j - (chain - 1), c])

    def item(t, lag, then):
        u = t - lag
        n = jnp.maximum(u, 0)
        k, c = lax.div(n, spacing), lax.rem(n, spacing)

        @pl.when((u >= 0) & (k < chain) & (c < chunks))
        def _():
            then(k, c)

    def each_sum(k, action):
        stop = jnp.where(k == chain - 1, blocks - 1, k + 1)

        @pl.loop(k, stop)
        def _(j):
            action(j)

    def z_part(t, h):
        def inward_part(k, c):
            if zhalf > 1:
                @pl.when(z_end > 0)
                def _():
                    z_inward(c, h).wait_recv()
                    zval[c, z_rows(h)] += zin[c, z_rows(h)]

                @pl.when(z_mid > 0)
                def _():
                    z_inward(c, h).start()

            @pl.when(z_mid == 0)
            def _():
                z_to_middle(k, c, h).start()

        def outward_part(k, c):
            z_to_middle(k, c, h).wait_recv()

            @pl.when(z_mid == 0)
            def _():
                zmid[lax.rem(k, 2), c, z_rows(h)] += zval[c, z_rows(h)]

            if zhalf > 1:
                @pl.when(z_end > 0)
                def _():
                    z_outward(k, c, h).start()

        item(t, z_end, inward_part)
        item(t, zhalf + z_mid, outward_part)

    def x_part(t):
        def inward_part(k, c):
            def one(j):
                x_first(j, c).wait_recv()
                acc[j, c, own] += x1[tail(j), c]
                if xhalf > 1:
                    @pl.when(x_end > 0)
                    def _():
                        x_inward(j, c).wait_recv()
                        acc[j, c, own] += xin[j, c]

                    @pl.when(x_mid > 0)
                    def _():
                        x_inward(j, c).start()

                @pl.when(x_mid == 0)
                def _():
                    x_to_middle(j, c).start()

            each_sum(k, one)

        def outward_part(k, c):
            def one(j):
                x_to_middle(j, c).wait_recv()

                @pl.when(x_mid == 0)
                def _():
                    x2[j, c] += acc[j, c, own]

                x_back(j, c).start()
                if xhalf > 1:
                    @pl.when(x_end > 0)
                    def _():
                        x_outward(j, c).start()

            each_sum(k, one)

        def last_part(k, c):
            def one(j):
                x_back(j, c).wait_recv()
                x_first(j, c).wait_send()
                x_to_middle(j, c).wait_send()
                x_back(j, c).wait_send()
                if xhalf > 1:
                    @pl.when(x_end > 0)
                    def _():
                        x_outward(j, c).wait_send()

                @pl.when(k == chain - 1)
                def _():
                    trailing_own(j, c).start()
                    trailing_other(j, c).start()

            each_sum(k, one)

        item(t, x_at + x_end, inward_part)
        item(t, x_at + xhalf + x_mid, outward_part)
        item(t, last_at, last_part)

    def value_part(k, c):
        @pl.when(c == 0)
        def _():
            for step in range(1, rhs_n):
                inv_copy(k, step).wait()
            inv_own(k).wait()

            @pl.when(k + 1 < chain)
            def _():
                inv_start(k + 1)

            inv_hi[k], inv_lo[k] = split(inv_land[k])

        @pl.when(k == 0)
        def _():
            set_pair(pl.ds(0, mr), first[c])

        @pl.when(k > 0)
        def _():
            before = jnp.maximum(k - 1, 0)
            set_pair(own, x2[before, c])
            set_pair(other, x3[0, c])

        zval[c] = product(inv_hi[k], inv_lo[k], mr)

    def update_part(k, c):
        solved_copy(k, c).start()
        for h in range(2):
            z_inward(c, h).wait_send()
        set_pair(pl.ds(0, mc), zmid[lax.rem(k, 2), c])

        @pl.loop(k + 1, jnp.where(k == chain - 1, blocks, k + 2))
        def _(i):
            spot = place(k, i)
            acc[i - 1, c] -= product(low_hi[spot], low_lo[spot], mc)
            x_first(i - 1, c).start()

        @pl.when(k < chain - 1)
        def _():
            for odd in range(2):
                @pl.when(lax.rem(c, 2) == odd)
                def _():
                    duo[:, odd * width:(odd + 1) * width] = pair[:mc, :width]
                    duo[:, (odd + 2) * width:(odd + 3) * width] = pair[:mc, width:]

            @pl.when(lax.rem(c, 2) == 1)
            def _():
                update_two(k, c, k + 2, jnp.minimum(k + 4, blocks))

    def update_two(k, c, begin, end):
        before = jnp.maximum(c - 1, 0)

        @pl.loop(begin, end)
        def _(i):
            spot = place(k, i)
            wide = jnp.dot(low_hi[spot], duo[...], preferred_element_type=jnp.float32)
            rest = jnp.dot(low_lo[spot], duo[:, :2 * width], preferred_element_type=jnp.float32)
            both = wide[:, :2 * width] + (wide[:, 2 * width:] + rest)
            acc[i - 1, before] -= both[:, :width]
            acc[i - 1, c] -= both[:, width:]

    def rest_part(k, c):
        @pl.when((k < chain - 1) & (lax.rem(c, 2) == 1))
        def _():
            update_two(k, c, k + 4, jnp.maximum(blocks, k + 4))

    def release_part(k, c):
        solved_copy(k, c).wait()
        if zhalf > 1:
            @pl.when(z_end > 0)
            def _():
                for h in range(2):
                    z_outward(k, c, h).wait_send()

    @pl.loop(0, slots + 1)
    def _(n):
        t = n - 1
        z_part(t, 0)
        x_part(t)
        item(t, -1, value_part)
        z_part(t, 1)
        item(t, solved_at + 1, release_part)

        @pl.when((t == 0) & (me_col == 0))
        def _():
            each_acc(lambda j, c: acc_copy(j, c).wait())

        item(t, solved_at + 1, rest_part)
        item(t, solved_at, update_part)
        take_block(t + 2)

    @pl.loop(0, (blocks - chain) * chunks)
    def _(n):
        j, c = chain - 1 + lax.div(n, chunks), lax.rem(n, chunks)
        trailing_own(j, c).wait()
        trailing_other(j, c).wait()


def hand_over(solved, trailing, solved_out, trailing_out, solved_buf, trailing_buf, solved_sem, trailing_sem):
    jobs = []
    for src, buf, dst, sems in (
        (solved, solved_buf, solved_out, solved_sem), (trailing, trailing_buf, trailing_out, trailing_sem),
    ):
        rows = src.shape[1] // 2
        for k in range(src.shape[0]):
            for half in range(2):
                at = pl.ds(half * rows, rows)
                jobs.append((
                    pltpu.make_async_copy(src.at[k, at], buf.at[k, at], sems.at[0, k, half]),
                    pltpu.make_async_copy(buf.at[k, at], dst.at[k, at], sems.at[1, k, half]),
                ))
    for come, _ in jobs:
        come.start()
    for come, go in jobs:
        come.wait()
        go.start()
    for _, go in jobs:
        go.wait()


def on_device(mesh, lower, inverse, right):
    rows_n, cols_n, rhs_n = mesh.shape["row"], mesh.shape["col"], mesh.shape["rhs"]
    blocks, mr, chain, mc = lower.shape
    width = LANES
    chunks = right.shape[2] // width
    assert chunks % 2 == 0
    part = inverse.shape[1]
    pairs = sum(blocks - 1 - k for k in range(chain))
    sums = blocks - 1
    stages = min(4, pairs)
    tails = blocks - chain
    mrh = mr // 2
    f32, bf16 = jnp.float32, jnp.bfloat16
    far = sums if cols_n > 4 else 1
    far_chunks = chunks if cols_n > 4 else 1
    dma = pltpu.SemaphoreType.DMA
    scratch = [
        pltpu.VMEM((pairs, mr, mc), bf16),
        pltpu.VMEM((pairs, mr, mc), bf16),
        pltpu.VMEM((chain, mc, mr), bf16),
        pltpu.VMEM((chain, mc, mr), bf16),
        pltpu.VMEM((stages, mr, mc), f32),
        pltpu.VMEM((chain, mc, mr), f32),
        pltpu.VMEM((chunks, mr, width), f32),
        pltpu.VMEM((sums, chunks, mr, width), f32),
        pltpu.VMEM((chunks, mc, width), f32),
        pltpu.VMEM((chunks, mc, width), f32),
        pltpu.VMEM((2, chunks, mc, width), f32),
        pltpu.VMEM((tails, chunks, mrh, width), f32),
        pltpu.VMEM((sums, chunks, mrh, width), f32),
        pltpu.VMEM((tails, chunks, mrh, width), f32),
        pltpu.VMEM((far, far_chunks, mrh, width), f32),
        pltpu.VMEM((max(mr, mc), 2 * width), bf16),
        pltpu.VMEM((mc, 4 * width), bf16),
        dma((stages,)),
        dma((chunks,)),
        dma((sums, chunks)),
        dma((chain,)),
        dma((chain, rhs_n - 1)),
        dma((chain, rhs_n - 1)),
        dma((chunks, 2)),
        dma((2, chunks, 2)),
        dma((chunks, 2)),
        dma((chunks, 2)),
        dma((chunks,)),
        dma((sums, chunks)),
        dma((sums, chunks)),
        dma((far, far_chunks)),
        dma((sums, chunks)),
        dma((sums, chunks)),
        dma((sums, chunks)),
        dma((sums, chunks)),
        dma((sums, chunks)),
        dma((2, tails, chunks)),
    ]
    dims = (rows_n, cols_n, rhs_n, chain, blocks, chunks, width)
    any_spec = pl.BlockSpec(memory_space=pl.ANY)
    found = pl.pallas_call(
        functools.partial(kernel, dims),
        out_shape=(
            jax.ShapeDtypeStruct((chain, mc, right.shape[2]), f32),
            jax.ShapeDtypeStruct((tails, mr, right.shape[2]), f32),
        ),
        in_specs=[any_spec] * 3,
        out_specs=(any_spec, any_spec),
        scratch_shapes=scratch,
        compiler_params=pltpu.CompilerParams(
            collective_id=0, has_side_effects=True, vmem_limit_bytes=62 * 1024 * 1024
        ),
        cost_estimate=pl.CostEstimate(
            flops=6 * (pairs + chain) * mr * mc * right.shape[2], bytes_accessed=4 * lower.size * 2, transcendentals=0
        ),
    )(lower, inverse, right)
    shapes = tuple(jax.ShapeDtypeStruct(array.shape, array.dtype) for array in found)
    return pl.pallas_call(
        hand_over,
        out_shape=shapes,
        in_specs=[any_spec] * 2,
        out_specs=(any_spec, any_spec),
        scratch_shapes=[
            *(pltpu.VMEM(shape.shape, shape.dtype) for shape in shapes),
            dma((2, chain, 2)),
            dma((2, tails, 2)),
        ],
        compiler_params=pltpu.CompilerParams(vmem_limit_bytes=62 * 1024 * 1024),
        cost_estimate=pl.CostEstimate(
            flops=0, bytes_accessed=8 * sum(array.size for array in found), transcendentals=0
        ),
    )(*found)


def solution(mesh):
    placed = (P(None, "row", None, "col"), P(None, ("col", "rhs"), "row"), P(None, "row", "rhs"))
    return jax.shard_map(
        functools.partial(on_device, mesh),
        mesh=mesh,
        in_specs=placed,
        out_specs=(P(None, "col", "rhs"), P(None, "row", "rhs")),
        check_vma=False,
    )
```

```python
import functools

import jax
import jax.numpy as jnp
from jax import lax
from jax.experimental import pallas as pl
from jax.experimental.pallas import tpu as pltpu
from jax.sharding import PartitionSpec as P

MESH = pl.DeviceIdType.MESH
LANES = 128
PARTS = 4


def split(value):
    high = value.astype(jnp.bfloat16)
    return high, (value - high.astype(jnp.float32)).astype(jnp.bfloat16)


def line_role(place, count):
    half = count // 2
    left = place < half
    inward = jnp.where(left, place + 1, place - 1)
    outward = jnp.where(left, place - 1, place + 1)
    from_end = jnp.where(left, place, count - 1 - place)
    return inward, outward, from_end, half - 1 - from_end


def kernel(
    dims, lower, inverse, right, solved, trailing,
    low_hi, low_lo, inv_hi, inv_lo, stage, inv_land, first, acc, zval, zin, zmid, x1, x2, x3, xin, pair, duo,
    stage_sem, first_sem, acc_sem, inv_own_sem, inv_send, inv_recv,
    zin_recv, zmid_recv, z_in_send, z_out_send, sol_sem,
    x1_send, x1_recv, xin_recv, x2_recv, x_in_send, x_out_send, x3_send, x3_recv, tra_sem,
):
    rows_n, cols_n, rhs_n, chain, blocks, chunks, width = dims
    line_n = cols_n // 2
    zhalf, xhalf = rows_n // 2, line_n // 2
    mr, mc = acc.shape[2], zval.shape[1]
    mrh, mch = mr // 2, mc // PARTS
    solved_at = rows_n - 1
    x_at = solved_at + 1
    last_at = x_at + line_n
    spacing = max(chunks, last_at + 1)
    slots = (chain - 1) * spacing + chunks + last_at

    me_row, me_col, me_rhs = lax.axis_index("row"), lax.axis_index("col"), lax.axis_index("rhs")
    core, chip = lax.rem(me_col, 2), lax.div(me_col, 2)
    sibling = me_col + 1 - 2 * core
    z_in, z_out, z_end, z_mid = line_role(me_row, rows_n)
    xc_in, xc_out, x_end, x_mid = line_role(chip, line_n)
    x_in, x_out = xc_in * 2 + core, xc_out * 2 + core
    own = pl.ds(pl.multiple_of(core * mrh, mrh), mrh)
    other = pl.ds(pl.multiple_of((1 - core) * mrh, mrh), mrh)

    barrier = pltpu.get_barrier_semaphore()

    def greet(device):
        pl.semaphore_signal(barrier, inc=1, device_id=device, device_id_type=MESH)

    greet({"row": z_in})
    greet({"col": sibling})
    greet({"col": x_in})
    for step in range(1, rhs_n):
        greet({"rhs": lax.rem(me_rhs + step, rhs_n)})
    if zhalf > 1:
        @pl.when(z_end > 0)
        def _():
            greet({"row": z_out})
    if xhalf > 1:
        @pl.when(x_end > 0)
        def _():
            greet({"col": x_out})
    count = 2 + rhs_n
    if zhalf > 1:
        count += (z_end > 0).astype(jnp.int32)
    if xhalf > 1:
        count += (x_end > 0).astype(jnp.int32)
    pl.semaphore_wait(barrier, count)

    def remote(src, dst, send, recv, device):
        return pltpu.make_async_remote_copy(
            src_ref=src, dst_ref=dst, send_sem=send, recv_sem=recv, device_id=device, device_id_type=MESH
        )

    part = inverse.shape[1]
    mine = pl.ds(pl.multiple_of(me_rhs * part, part), part)

    def inv_copy(k, step):
        return remote(
            inverse.at[k], inv_land.at[k, mine], inv_send.at[k, step - 1], inv_recv.at[k, step - 1],
            {"rhs": lax.rem(me_rhs + step, rhs_n)},
        )

    def inv_own(k):
        return pltpu.make_async_copy(inverse.at[k], inv_land.at[k, mine], inv_own_sem.at[k])

    def inv_start(k):
        for step in range(1, rhs_n):
            inv_copy(k, step).start()
        inv_own(k).start()

    inv_start(0)

    def columns(c):
        return pl.ds(pl.multiple_of(c * width, width), width)

    def first_copy(c):
        return pltpu.make_async_copy(right.at[0, :, columns(c)], first.at[c], first_sem.at[c])

    def acc_copy(j, c):
        return pltpu.make_async_copy(right.at[j + 1, :, columns(c)], acc.at[j, c], acc_sem.at[j, c])

    def each_acc(action):
        @pl.loop(0, (blocks - 1) * chunks)
        def _(n):
            action(lax.div(n, chunks), lax.rem(n, chunks))

    @pl.loop(0, chunks)
    def _(c):
        first_copy(c).start()

    pairs, slot_n = low_hi.shape[0], stage.shape[0]

    def place(k, i):
        return k * (blocks - 1) - lax.div(k * (k - 1), 2) + i - k - 1

    def stage_copy(spot, action):
        for k in range(chain):
            begin = k * (blocks - 1) - (k * (k - 1)) // 2
            end = begin + blocks - 1 - k

            @pl.when((spot >= begin) & (spot < end))
            def _():
                at = lax.rem(spot, slot_n)
                action(pltpu.make_async_copy(lower.at[spot - begin + k + 1, :, k, :], stage.at[at], stage_sem.at[at]))

    def take_block(spot):
        @pl.when((spot >= 0) & (spot < pairs))
        def _():
            stage_copy(spot, lambda copy: copy.wait())
            low_hi[spot], low_lo[spot] = split(stage[lax.rem(spot, slot_n)])

            @pl.when(spot + slot_n < pairs)
            def _():
                stage_copy(spot + slot_n, lambda copy: copy.start())

    @pl.loop(0, min(slot_n, pairs))
    def _(spot):
        stage_copy(spot, lambda copy: copy.start())

    @pl.when(me_col == 0)
    def _():
        each_acc(lambda j, c: acc_copy(j, c).start())

    @pl.when(me_col != 0)
    def _():
        def clear(j, c):
            acc[j, c] = jnp.zeros((mr, width), jnp.float32)

        each_acc(clear)

    take_block(0)

    @pl.loop(0, chunks)
    def _(c):
        first_copy(c).wait()

    def product(high, low, depth):
        both = jnp.dot(high, pair[:depth, :], preferred_element_type=jnp.float32)
        rest = jnp.dot(low, pair[:depth, :width], preferred_element_type=jnp.float32)
        return both[:, :width] + (both[:, width:] + rest)

    def set_pair(rows, value):
        high, low = split(value)
        pair[rows, :width] = high
        pair[rows, width:] = low

    def z_rows(h):
        return pl.ds(h * mch, mch)

    def z_to_middle(k, c, h):
        return remote(zval.at[c, z_rows(h)], zmid.at[lax.rem(k, 2), c, z_rows(h)], z_in_send.at[c, h],
                      zmid_recv.at[lax.rem(k, 2), c, h], {"row": z_in})

    def z_inward(c, h):
        return remote(zval.at[c, z_rows(h)], zin.at[c, z_rows(h)], z_in_send.at[c, h], zin_recv.at[c, h], {"row": z_in})

    def z_outward(k, c, h):
        at = zmid.at[lax.rem(k, 2), c, z_rows(h)]
        return remote(at, at, z_out_send.at[c, h], zmid_recv.at[lax.rem(k, 2), c, h], {"row": z_out})

    def tail(j):
        return jnp.maximum(j - (chain - 1), 0)

    def x_first(j, c):
        return remote(acc.at[j, c, other], x1.at[tail(j), c], x1_send.at[j, c], x1_recv.at[j, c], {"col": sibling})

    def x_to_middle(j, c):
        return remote(acc.at[j, c, own], x2.at[j, c], x_in_send.at[j, c], x2_recv.at[j, c], {"col": x_in})

    def x_inward(j, c):
        return remote(acc.at[j, c, own], xin.at[j, c], x_in_send.at[j, c], xin_recv.at[j, c], {"col": x_in})

    def x_outward(j, c):
        return remote(x2.at[j, c], x2.at[j, c], x_out_send.at[j, c], x2_recv.at[j, c], {"col": x_out})

    def x_back(j, c):
        return remote(x2.at[j, c], x3.at[tail(j), c], x3_send.at[j, c], x3_recv.at[j, c], {"col": sibling})

    def solved_copy(k, c):
        return pltpu.make_async_copy(zmid.at[lax.rem(k, 2), c], solved.at[k, :, columns(c)], sol_sem.at[c])

    def trailing_own(j, c):
        return pltpu.make_async_copy(
            x2.at[j, c], trailing.at[j - (chain - 1), own, columns(c)], tra_sem.at[0, j - (chain - 1), c])

    def trailing_other(j, c):
        return pltpu.make_async_copy(
            x3.at[tail(j), c], trailing.at[j - (chain - 1), other, columns(c)], tra_sem.at[1, j - (chain - 1), c])

    def item(t, lag, then):
        u = t - lag
        n = jnp.maximum(u, 0)
        k, c = lax.div(n, spacing), lax.rem(n, spacing)

        @pl.when((u >= 0) & (k < chain) & (c < chunks))
        def _():
            then(k, c)

    def each_sum(k, action):
        stop = jnp.where(k == chain - 1, blocks - 1, k + 1)

        @pl.loop(k, stop)
        def _(j):
            action(j)

    def z_part(t, h):
        def inward_part(k, c):
            if zhalf > 1:
                @pl.when(z_end > 0)
                def _():
                    z_inward(c, h).wait_recv()
                    zval[c, z_rows(h)] += zin[c, z_rows(h)]

                @pl.when(z_mid > 0)
                def _():
                    z_inward(c, h).start()

            @pl.when(z_mid == 0)
            def _():
                z_to_middle(k, c, h).start()

        def outward_part(k, c):
            z_to_middle(k, c, h).wait_recv()

            @pl.when(z_mid == 0)
            def _():
                zmid[lax.rem(k, 2), c, z_rows(h)] += zval[c, z_rows(h)]

            if zhalf > 1:
                @pl.when(z_end > 0)
                def _():
                    z_outward(k, c, h).start()

        item(t, z_end, inward_part)
        item(t, zhalf + z_mid, outward_part)

    def x_part(t):
        def inward_part(k, c):
            def one(j):
                x_first(j, c).wait_recv()
                acc[j, c, own] += x1[tail(j), c]
                if xhalf > 1:
                    @pl.when(x_end > 0)
                    def _():
                        x_inward(j, c).wait_recv()
                        acc[j, c, own] += xin[j, c]

                    @pl.when(x_mid > 0)
                    def _():
                        x_inward(j, c).start()

                @pl.when(x_mid == 0)
                def _():
                    x_to_middle(j, c).start()

            each_sum(k, one)

        def outward_part(k, c):
            def one(j):
                x_to_middle(j, c).wait_recv()

                @pl.when(x_mid == 0)
                def _():
                    x2[j, c] += acc[j, c, own]

                x_back(j, c).start()
                if xhalf > 1:
                    @pl.when(x_end > 0)
                    def _():
                        x_outward(j, c).start()

            each_sum(k, one)

        def last_part(k, c):
            def one(j):
                x_back(j, c).wait_recv()
                x_first(j, c).wait_send()
                x_to_middle(j, c).wait_send()
                x_back(j, c).wait_send()
                if xhalf > 1:
                    @pl.when(x_end > 0)
                    def _():
                        x_outward(j, c).wait_send()

                @pl.when(k == chain - 1)
                def _():
                    trailing_own(j, c).start()
                    trailing_other(j, c).start()

            each_sum(k, one)

        item(t, x_at + x_end, inward_part)
        item(t, x_at + xhalf + x_mid, outward_part)
        item(t, last_at, last_part)

    def value_part(k, c):
        @pl.when(c == 0)
        def _():
            for step in range(1, rhs_n):
                inv_copy(k, step).wait()
            inv_own(k).wait()

            @pl.when(k + 1 < chain)
            def _():
                inv_start(k + 1)

            inv_hi[k], inv_lo[k] = split(inv_land[k])

        @pl.when(k == 0)
        def _():
            set_pair(pl.ds(0, mr), first[c])

        @pl.when(k > 0)
        def _():
            before = jnp.maximum(k - 1, 0)
            set_pair(own, x2[before, c])
            set_pair(other, x3[0, c])

        zval[c] = product(inv_hi[k], inv_lo[k], mr)

    def update_part(k, c):
        solved_copy(k, c).start()
        for h in range(PARTS):
            z_inward(c, h).wait_send()
        set_pair(pl.ds(0, mc), zmid[lax.rem(k, 2), c])

        @pl.loop(k + 1, jnp.where(k == chain - 1, blocks, k + 2))
        def _(i):
            spot = place(k, i)
            acc[i - 1, c] -= product(low_hi[spot], low_lo[spot], mc)
            x_first(i - 1, c).start()

    def far_part(k, c):
        @pl.when(k < chain - 1)
        def _():
            for odd in range(2):
                @pl.when(lax.rem(c, 2) == odd)
                def _():
                    duo[:, odd * width:(odd + 1) * width] = pair[:mc, :width]
                    duo[:, (odd + 2) * width:(odd + 3) * width] = pair[:mc, width:]

            @pl.when(lax.rem(c, 2) == 1)
            def _():
                update_two(k, c, k + 2, jnp.minimum(k + 4, blocks))

    def update_two(k, c, begin, end):
        before = jnp.maximum(c - 1, 0)

        @pl.loop(begin, end)
        def _(i):
            spot = place(k, i)
            wide = jnp.dot(low_hi[spot], duo[...], preferred_element_type=jnp.float32)
            rest = jnp.dot(low_lo[spot], duo[:, :2 * width], preferred_element_type=jnp.float32)
            both = wide[:, :2 * width] + (wide[:, 2 * width:] + rest)
            acc[i - 1, before] -= both[:, :width]
            acc[i - 1, c] -= both[:, width:]

    def rest_part(k, c):
        @pl.when((k < chain - 1) & (lax.rem(c, 2) == 1))
        def _():
            update_two(k, c, k + 4, jnp.maximum(blocks, k + 4))

    def release_part(k, c):
        solved_copy(k, c).wait()
        if zhalf > 1:
            @pl.when(z_end > 0)
            def _():
                for h in range(PARTS):
                    z_outward(k, c, h).wait_send()

    @pl.loop(0, slots + 1)
    def _(n):
        t = n - 1
        for h in range(PARTS // 2):
            z_part(t, h)
        x_part(t)
        item(t, -1, value_part)
        item(t, solved_at + 1, rest_part)
        for h in range(PARTS // 2, PARTS):
            z_part(t, h)
        item(t, solved_at + 1, release_part)

        @pl.when((t == 0) & (me_col == 0))
        def _():
            each_acc(lambda j, c: acc_copy(j, c).wait())

        item(t, solved_at, update_part)
        item(t, solved_at, far_part)
        take_block(t + 2)

    @pl.loop(0, (blocks - chain) * chunks)
    def _(n):
        j, c = chain - 1 + lax.div(n, chunks), lax.rem(n, chunks)
        trailing_own(j, c).wait()
        trailing_other(j, c).wait()


def hand_over(solved, trailing, solved_out, trailing_out, solved_buf, trailing_buf, solved_sem, trailing_sem):
    jobs = []
    for src, buf, dst, sems in (
        (solved, solved_buf, solved_out, solved_sem), (trailing, trailing_buf, trailing_out, trailing_sem),
    ):
        rows = src.shape[1] // 2
        for k in range(src.shape[0]):
            for half in range(2):
                at = pl.ds(half * rows, rows)
                jobs.append((
                    pltpu.make_async_copy(src.at[k, at], buf.at[k, at], sems.at[0, k, half]),
                    pltpu.make_async_copy(buf.at[k, at], dst.at[k, at], sems.at[1, k, half]),
                ))
    for come, _ in jobs:
        come.start()
    for come, go in jobs:
        come.wait()
        go.start()
    for _, go in jobs:
        go.wait()


def on_device(mesh, lower, inverse, right):
    rows_n, cols_n, rhs_n = mesh.shape["row"], mesh.shape["col"], mesh.shape["rhs"]
    blocks, mr, chain, mc = lower.shape
    width = LANES
    chunks = right.shape[2] // width
    assert chunks % 2 == 0
    part = inverse.shape[1]
    pairs = sum(blocks - 1 - k for k in range(chain))
    sums = blocks - 1
    stages = min(4, pairs)
    tails = blocks - chain
    mrh = mr // 2
    f32, bf16 = jnp.float32, jnp.bfloat16
    far = sums if cols_n > 4 else 1
    far_chunks = chunks if cols_n > 4 else 1
    dma = pltpu.SemaphoreType.DMA
    scratch = [
        pltpu.VMEM((pairs, mr, mc), bf16),
        pltpu.VMEM((pairs, mr, mc), bf16),
        pltpu.VMEM((chain, mc, mr), bf16),
        pltpu.VMEM((chain, mc, mr), bf16),
        pltpu.VMEM((stages, mr, mc), f32),
        pltpu.VMEM((chain, mc, mr), f32),
        pltpu.VMEM((chunks, mr, width), f32),
        pltpu.VMEM((sums, chunks, mr, width), f32),
        pltpu.VMEM((chunks, mc, width), f32),
        pltpu.VMEM((chunks, mc, width), f32),
        pltpu.VMEM((2, chunks, mc, width), f32),
        pltpu.VMEM((tails, chunks, mrh, width), f32),
        pltpu.VMEM((sums, chunks, mrh, width), f32),
        pltpu.VMEM((tails, chunks, mrh, width), f32),
        pltpu.VMEM((far, far_chunks, mrh, width), f32),
        pltpu.VMEM((max(mr, mc), 2 * width), bf16),
        pltpu.VMEM((mc, 4 * width), bf16),
        dma((stages,)),
        dma((chunks,)),
        dma((sums, chunks)),
        dma((chain,)),
        dma((chain, rhs_n - 1)),
        dma((chain, rhs_n - 1)),
        dma((chunks, PARTS)),
        dma((2, chunks, PARTS)),
        dma((chunks, PARTS)),
        dma((chunks, PARTS)),
        dma((chunks,)),
        dma((sums, chunks)),
        dma((sums, chunks)),
        dma((far, far_chunks)),
        dma((sums, chunks)),
        dma((sums, chunks)),
        dma((sums, chunks)),
        dma((sums, chunks)),
        dma((sums, chunks)),
        dma((2, tails, chunks)),
    ]
    dims = (rows_n, cols_n, rhs_n, chain, blocks, chunks, width)
    any_spec = pl.BlockSpec(memory_space=pl.ANY)
    found = pl.pallas_call(
        functools.partial(kernel, dims),
        out_shape=(
            jax.ShapeDtypeStruct((chain, mc, right.shape[2]), f32),
            jax.ShapeDtypeStruct((tails, mr, right.shape[2]), f32),
        ),
        in_specs=[any_spec] * 3,
        out_specs=(any_spec, any_spec),
        scratch_shapes=scratch,
        compiler_params=pltpu.CompilerParams(
            collective_id=0, has_side_effects=True, vmem_limit_bytes=62 * 1024 * 1024
        ),
        cost_estimate=pl.CostEstimate(
            flops=6 * (pairs + chain) * mr * mc * right.shape[2], bytes_accessed=4 * lower.size * 2, transcendentals=0
        ),
    )(lower, inverse, right)
    shapes = tuple(jax.ShapeDtypeStruct(array.shape, array.dtype) for array in found)
    return pl.pallas_call(
        hand_over,
        out_shape=shapes,
        in_specs=[any_spec] * 2,
        out_specs=(any_spec, any_spec),
        scratch_shapes=[
            *(pltpu.VMEM(shape.shape, shape.dtype) for shape in shapes),
            dma((2, chain, 2)),
            dma((2, tails, 2)),
        ],
        compiler_params=pltpu.CompilerParams(vmem_limit_bytes=62 * 1024 * 1024),
        cost_estimate=pl.CostEstimate(
            flops=0, bytes_accessed=8 * sum(array.size for array in found), transcendentals=0
        ),
    )(*found)


def solution(mesh):
    placed = (P(None, "row", None, "col"), P(None, ("col", "rhs"), "row"), P(None, "row", "rhs"))
    return jax.shard_map(
        functools.partial(on_device, mesh),
        mesh=mesh,
        in_specs=placed,
        out_specs=(P(None, "col", "rhs"), P(None, "row", "rhs")),
        check_vma=False,
    )
```

```python
import functools

import jax
import jax.numpy as jnp
from jax import lax
from jax.experimental import pallas as pl
from jax.experimental.pallas import tpu as pltpu
from jax.sharding import PartitionSpec as P

MESH = pl.DeviceIdType.MESH
LANES = 128
PARTS = 4
EARLY = 2


def split(value):
    high = value.astype(jnp.bfloat16)
    return high, (value - high.astype(jnp.float32)).astype(jnp.bfloat16)


def line_role(place, count):
    half = count // 2
    left = place < half
    inward = jnp.where(left, place + 1, place - 1)
    outward = jnp.where(left, place - 1, place + 1)
    from_end = jnp.where(left, place, count - 1 - place)
    return inward, outward, from_end, half - 1 - from_end


def kernel(
    dims, lower, inverse, right, solved, trailing,
    low_hi, low_lo, inv_hi, inv_lo, stage, inv_land, first, acc, zval, zin, zmid, x1, x2, x3, xin, pair, duo,
    stage_sem, first_sem, acc_sem, inv_own_sem, inv_send, inv_recv,
    zin_recv, zmid_recv, z_in_send, z_out_send, sol_sem,
    x1_send, x1_recv, xin_recv, x2_recv, x_in_send, x_out_send, x3_send, x3_recv, tra_sem,
):
    rows_n, cols_n, rhs_n, chain, blocks, chunks, width = dims
    line_n = cols_n // 2
    zhalf, xhalf = rows_n // 2, line_n // 2
    mr, mc = acc.shape[2], zval.shape[1]
    mrh, mch = mr // 2, mc // PARTS
    solved_at = rows_n - 1
    x_at = solved_at + 1
    last_at = x_at + line_n
    spacing = max(chunks, last_at + 1)
    slots = (chain - 1) * spacing + chunks + last_at

    me_row, me_col, me_rhs = lax.axis_index("row"), lax.axis_index("col"), lax.axis_index("rhs")
    core, chip = lax.rem(me_col, 2), lax.div(me_col, 2)
    sibling = me_col + 1 - 2 * core
    z_in, z_out, z_end, z_mid = line_role(me_row, rows_n)
    xc_in, xc_out, x_end, x_mid = line_role(chip, line_n)
    x_in, x_out = xc_in * 2 + core, xc_out * 2 + core
    own = pl.ds(pl.multiple_of(core * mrh, mrh), mrh)
    other = pl.ds(pl.multiple_of((1 - core) * mrh, mrh), mrh)

    barrier = pltpu.get_barrier_semaphore()

    def greet(device):
        pl.semaphore_signal(barrier, inc=1, device_id=device, device_id_type=MESH)

    greet({"row": z_in})
    greet({"col": sibling})
    greet({"col": x_in})
    for step in range(1, rhs_n):
        greet({"rhs": lax.rem(me_rhs + step, rhs_n)})
    if zhalf > 1:
        @pl.when(z_end > 0)
        def _():
            greet({"row": z_out})
    if xhalf > 1:
        @pl.when(x_end > 0)
        def _():
            greet({"col": x_out})
    count = 2 + rhs_n
    if zhalf > 1:
        count += (z_end > 0).astype(jnp.int32)
    if xhalf > 1:
        count += (x_end > 0).astype(jnp.int32)
    pl.semaphore_wait(barrier, count)

    def remote(src, dst, send, recv, device):
        return pltpu.make_async_remote_copy(
            src_ref=src, dst_ref=dst, send_sem=send, recv_sem=recv, device_id=device, device_id_type=MESH
        )

    part = inverse.shape[1]
    mine = pl.ds(pl.multiple_of(me_rhs * part, part), part)

    def inv_copy(k, step):
        return remote(
            inverse.at[k], inv_land.at[k, mine], inv_send.at[k, step - 1], inv_recv.at[k, step - 1],
            {"rhs": lax.rem(me_rhs + step, rhs_n)},
        )

    def inv_own(k):
        return pltpu.make_async_copy(inverse.at[k], inv_land.at[k, mine], inv_own_sem.at[k])

    def inv_start(k):
        for step in range(1, rhs_n):
            inv_copy(k, step).start()
        inv_own(k).start()

    inv_start(0)

    def columns(c):
        return pl.ds(pl.multiple_of(c * width, width), width)

    def first_copy(c):
        return pltpu.make_async_copy(right.at[0, :, columns(c)], first.at[c], first_sem.at[c])

    def acc_copy(j, c):
        return pltpu.make_async_copy(right.at[j + 1, :, columns(c)], acc.at[j, c], acc_sem.at[j, c])

    def each_acc(action):
        @pl.loop(0, (blocks - 1) * chunks)
        def _(n):
            action(lax.div(n, chunks), lax.rem(n, chunks))

    @pl.loop(0, chunks)
    def _(c):
        first_copy(c).start()

    pairs, slot_n = low_hi.shape[0], stage.shape[0]

    def place(k, i):
        return k * (blocks - 1) - lax.div(k * (k - 1), 2) + i - k - 1

    def stage_copy(spot, action):
        for k in range(chain):
            begin = k * (blocks - 1) - (k * (k - 1)) // 2
            end = begin + blocks - 1 - k

            @pl.when((spot >= begin) & (spot < end))
            def _():
                at = lax.rem(spot, slot_n)
                action(pltpu.make_async_copy(lower.at[spot - begin + k + 1, :, k, :], stage.at[at], stage_sem.at[at]))

    def take_block(spot):
        @pl.when((spot >= 0) & (spot < pairs))
        def _():
            stage_copy(spot, lambda copy: copy.wait())
            low_hi[spot], low_lo[spot] = split(stage[lax.rem(spot, slot_n)])

            @pl.when(spot + slot_n < pairs)
            def _():
                stage_copy(spot + slot_n, lambda copy: copy.start())

    @pl.loop(0, min(slot_n, pairs))
    def _(spot):
        stage_copy(spot, lambda copy: copy.start())

    @pl.loop(0, chunks)
    def _(c):
        first_copy(c).wait()

    def product(high, low, depth):
        both = jnp.dot(high, pair[:depth, :], preferred_element_type=jnp.float32)
        rest = jnp.dot(low, pair[:depth, :width], preferred_element_type=jnp.float32)
        return both[:, :width] + (both[:, width:] + rest)

    def set_pair(rows, value):
        high, low = split(value)
        pair[rows, :width] = high
        pair[rows, width:] = low

    own_parts = PARTS // rhs_n

    def z_rows(h):
        at = lax.rem(h + me_rhs * own_parts, PARTS)
        return pl.ds(pl.multiple_of(at * mch, mch), mch)

    def z_to_middle(k, c, h):
        return remote(zval.at[c, z_rows(h)], zmid.at[lax.rem(k, 2), c, z_rows(h)], z_in_send.at[c, h],
                      zmid_recv.at[lax.rem(k, 2), c, h], {"row": z_in})

    def z_inward(c, h):
        return remote(zval.at[c, z_rows(h)], zin.at[c, z_rows(h)], z_in_send.at[c, h], zin_recv.at[c, h], {"row": z_in})

    def z_outward(k, c, h):
        at = zmid.at[lax.rem(k, 2), c, z_rows(h)]
        return remote(at, at, z_out_send.at[c, h], zmid_recv.at[lax.rem(k, 2), c, h], {"row": z_out})

    def tail(j):
        return jnp.maximum(j - (chain - 1), 0)

    def x_first(j, c):
        return remote(acc.at[j, c, other], x1.at[tail(j), c], x1_send.at[j, c], x1_recv.at[j, c], {"col": sibling})

    def x_to_middle(j, c):
        return remote(acc.at[j, c, own], x2.at[j, c], x_in_send.at[j, c], x2_recv.at[j, c], {"col": x_in})

    def x_inward(j, c):
        return remote(acc.at[j, c, own], xin.at[j, c], x_in_send.at[j, c], xin_recv.at[j, c], {"col": x_in})

    def x_outward(j, c):
        return remote(x2.at[j, c], x2.at[j, c], x_out_send.at[j, c], x2_recv.at[j, c], {"col": x_out})

    def x_back(j, c):
        return remote(x2.at[j, c], x3.at[tail(j), c], x3_send.at[j, c], x3_recv.at[j, c], {"col": sibling})

    def solved_copy(k, c):
        return pltpu.make_async_copy(zmid.at[lax.rem(k, 2), c], solved.at[k, :, columns(c)], sol_sem.at[c])

    def trailing_own(j, c):
        return pltpu.make_async_copy(
            x2.at[j, c], trailing.at[j - (chain - 1), own, columns(c)], tra_sem.at[0, j - (chain - 1), c])

    def trailing_other(j, c):
        return pltpu.make_async_copy(
            x3.at[tail(j), c], trailing.at[j - (chain - 1), other, columns(c)], tra_sem.at[1, j - (chain - 1), c])

    def item(t, lag, then):
        u = t - lag
        n = jnp.maximum(u, 0)
        k, c = lax.div(n, spacing), lax.rem(n, spacing)

        @pl.when((u >= 0) & (k < chain) & (c < chunks))
        def _():
            then(k, c)

    def each_sum(k, action):
        stop = jnp.where(k == chain - 1, blocks - 1, k + 1)

        @pl.loop(k, stop)
        def _(j):
            action(j)

    def z_steps(h):
        def inward_part(k, c):
            if zhalf > 1:
                @pl.when(z_end > 0)
                def _():
                    z_inward(c, h).wait_recv()
                    zval[c, z_rows(h)] += zin[c, z_rows(h)]

                @pl.when(z_mid > 0)
                def _():
                    z_inward(c, h).start()

            @pl.when(z_mid == 0)
            def _():
                z_to_middle(k, c, h).start()

        def outward_part(k, c):
            z_to_middle(k, c, h).wait_recv()

            @pl.when(z_mid == 0)
            def _():
                zmid[lax.rem(k, 2), c, z_rows(h)] += zval[c, z_rows(h)]

            if zhalf > 1:
                @pl.when(z_end > 0)
                def _():
                    z_outward(k, c, h).start()

        return inward_part, outward_part

    def z_part(t, h):
        for lag, step in zip((z_end, zhalf + z_mid), z_steps(h)):
            def once(k, c, step=step):
                if h >= own_parts:
                    step(k, c)
                else:
                    @pl.when((k > 0) | (c >= EARLY))
                    def _():
                        step(k, c)

            item(t, lag, once)

    def x_part(t):
        def inward_part(k, c):
            def one(j):
                x_first(j, c).wait_recv()
                acc[j, c, own] += x1[tail(j), c]
                if xhalf > 1:
                    @pl.when(x_end > 0)
                    def _():
                        x_inward(j, c).wait_recv()
                        acc[j, c, own] += xin[j, c]

                    @pl.when(x_mid > 0)
                    def _():
                        x_inward(j, c).start()

                @pl.when(x_mid == 0)
                def _():
                    x_to_middle(j, c).start()

            each_sum(k, one)

        def outward_part(k, c):
            def one(j):
                x_to_middle(j, c).wait_recv()

                @pl.when(x_mid == 0)
                def _():
                    x2[j, c] += acc[j, c, own]

                x_back(j, c).start()
                if xhalf > 1:
                    @pl.when(x_end > 0)
                    def _():
                        x_outward(j, c).start()

            each_sum(k, one)

        def last_part(k, c):
            def one(j):
                x_back(j, c).wait_recv()
                x_first(j, c).wait_send()
                x_to_middle(j, c).wait_send()
                x_back(j, c).wait_send()
                if xhalf > 1:
                    @pl.when(x_end > 0)
                    def _():
                        x_outward(j, c).wait_send()

                @pl.when(k == chain - 1)
                def _():
                    trailing_own(j, c).start()
                    trailing_other(j, c).start()

            each_sum(k, one)

        item(t, x_at + x_end, inward_part)
        item(t, x_at + xhalf + x_mid, outward_part)
        item(t, last_at, last_part)

    def value_part(k, c):
        @pl.when(c == 0)
        def _():
            for step in range(1, rhs_n):
                inv_copy(k, step).wait()

            @pl.when(k > 0)
            def _():
                inv_own(k).wait()

            @pl.when(k + 1 < chain)
            def _():
                inv_start(k + 1)

            inv_hi[k], inv_lo[k] = split(inv_land[k])

        @pl.when(k == 0)
        def _():
            set_pair(pl.ds(0, mr), first[c])

        @pl.when(k > 0)
        def _():
            before = jnp.maximum(k - 1, 0)
            set_pair(own, x2[before, c])
            set_pair(other, x3[0, c])

        @pl.when((k > 0) | (c >= EARLY))
        def _():
            zval[c] = product(inv_hi[k], inv_lo[k], mr)

        @pl.when((k == 0) & (c < EARLY))
        def _():
            for step in range(1, rhs_n):
                value_rows(0, c, lax.rem(me_rhs + step, rhs_n))

    def value_rows(k, c, group):
        rows = pl.ds(pl.multiple_of(group * part, part), part)
        zval[c, rows] = product(inv_hi[k, rows], inv_lo[k, rows], mr)

    def update_part(k, c):
        solved_copy(k, c).start()
        for h in range(PARTS):
            z_inward(c, h).wait_send()
        set_pair(pl.ds(0, mc), zmid[lax.rem(k, 2), c])

        @pl.loop(k + 1, jnp.where(k == chain - 1, blocks, k + 2))
        def _(i):
            spot = place(k, i)
            acc[i - 1, c] -= product(low_hi[spot], low_lo[spot], mc)
            x_first(i - 1, c).start()

    def far_part(k, c):
        @pl.when(k < chain - 1)
        def _():
            for odd in range(2):
                @pl.when(lax.rem(c, 2) == odd)
                def _():
                    duo[:, odd * width:(odd + 1) * width] = pair[:mc, :width]
                    duo[:, (odd + 2) * width:(odd + 3) * width] = pair[:mc, width:]

            @pl.when(lax.rem(c, 2) == 1)
            def _():
                update_two(k, c, k + 2, jnp.minimum(k + 4, blocks))

    def update_two(k, c, begin, end):
        before = jnp.maximum(c - 1, 0)

        @pl.loop(begin, end)
        def _(i):
            spot = place(k, i)
            wide = jnp.dot(low_hi[spot], duo[...], preferred_element_type=jnp.float32)
            rest = jnp.dot(low_lo[spot], duo[:, :2 * width], preferred_element_type=jnp.float32)
            both = wide[:, :2 * width] + (wide[:, 2 * width:] + rest)
            acc[i - 1, before] -= both[:, :width]
            acc[i - 1, c] -= both[:, width:]

    def rest_part(k, c):
        @pl.when((k < chain - 1) & (lax.rem(c, 2) == 1))
        def _():
            update_two(k, c, k + 4, jnp.maximum(blocks, k + 4))

    def release_part(k, c):
        solved_copy(k, c).wait()
        if zhalf > 1:
            @pl.when(z_end > 0)
            def _():
                for h in range(PARTS):
                    z_outward(k, c, h).wait_send()

    inv_own(0).wait()
    inv_hi[0, mine], inv_lo[0, mine] = split(inv_land[0, mine])
    for c in range(EARLY):
        set_pair(pl.ds(0, mr), first[c])
        value_rows(0, c, me_rhs)
        for h in range(own_parts):
            z_steps(h)[0](0, c)
    @pl.when(me_col == 0)
    def _():
        each_acc(lambda j, c: acc_copy(j, c).start())

    @pl.when(me_col != 0)
    def _():
        def clear(j, c):
            acc[j, c] = jnp.zeros((mr, width), jnp.float32)

        each_acc(clear)

    taken = min(4, pairs)
    for spot in range(taken):
        take_block(spot)
    for c in range(EARLY):
        for h in range(own_parts):
            z_steps(h)[1](0, c)

    @pl.loop(0, slots + 1)
    def _(n):
        t = n - 1
        for h in range(PARTS // 2):
            z_part(t, h)
        x_part(t)
        item(t, -1, value_part)
        item(t, solved_at + 1, rest_part)
        for h in range(PARTS // 2, PARTS):
            z_part(t, h)
        item(t, solved_at + 1, release_part)

        @pl.when((t == 0) & (me_col == 0))
        def _():
            each_acc(lambda j, c: acc_copy(j, c).wait())

        item(t, solved_at, update_part)
        item(t, solved_at, far_part)
        take_block(t + 1 + taken)

    @pl.loop(0, (blocks - chain) * chunks)
    def _(n):
        j, c = chain - 1 + lax.div(n, chunks), lax.rem(n, chunks)
        trailing_own(j, c).wait()
        trailing_other(j, c).wait()


def hand_over(solved, trailing, solved_out, trailing_out, solved_buf, trailing_buf, solved_sem, trailing_sem):
    jobs = []
    for src, buf, dst, sems in (
        (solved, solved_buf, solved_out, solved_sem), (trailing, trailing_buf, trailing_out, trailing_sem),
    ):
        rows = src.shape[1] // 2
        for k in range(src.shape[0]):
            for half in range(2):
                at = pl.ds(half * rows, rows)
                jobs.append((
                    pltpu.make_async_copy(src.at[k, at], buf.at[k, at], sems.at[0, k, half]),
                    pltpu.make_async_copy(buf.at[k, at], dst.at[k, at], sems.at[1, k, half]),
                ))
    for come, _ in jobs:
        come.start()
    for come, go in jobs:
        come.wait()
        go.start()
    for _, go in jobs:
        go.wait()


def on_device(mesh, lower, inverse, right):
    rows_n, cols_n, rhs_n = mesh.shape["row"], mesh.shape["col"], mesh.shape["rhs"]
    blocks, mr, chain, mc = lower.shape
    width = LANES
    chunks = right.shape[2] // width
    assert chunks % 2 == 0
    part = inverse.shape[1]
    pairs = sum(blocks - 1 - k for k in range(chain))
    sums = blocks - 1
    stages = min(4, pairs)
    tails = blocks - chain
    mrh = mr // 2
    f32, bf16 = jnp.float32, jnp.bfloat16
    far = sums if cols_n > 4 else 1
    far_chunks = chunks if cols_n > 4 else 1
    dma = pltpu.SemaphoreType.DMA
    scratch = [
        pltpu.VMEM((pairs, mr, mc), bf16),
        pltpu.VMEM((pairs, mr, mc), bf16),
        pltpu.VMEM((chain, mc, mr), bf16),
        pltpu.VMEM((chain, mc, mr), bf16),
        pltpu.VMEM((stages, mr, mc), f32),
        pltpu.VMEM((chain, mc, mr), f32),
        pltpu.VMEM((chunks, mr, width), f32),
        pltpu.VMEM((sums, chunks, mr, width), f32),
        pltpu.VMEM((chunks, mc, width), f32),
        pltpu.VMEM((chunks, mc, width), f32),
        pltpu.VMEM((2, chunks, mc, width), f32),
        pltpu.VMEM((tails, chunks, mrh, width), f32),
        pltpu.VMEM((sums, chunks, mrh, width), f32),
        pltpu.VMEM((tails, chunks, mrh, width), f32),
        pltpu.VMEM((far, far_chunks, mrh, width), f32),
        pltpu.VMEM((max(mr, mc), 2 * width), bf16),
        pltpu.VMEM((mc, 4 * width), bf16),
        dma((stages,)),
        dma((chunks,)),
        dma((sums, chunks)),
        dma((chain,)),
        dma((chain, rhs_n - 1)),
        dma((chain, rhs_n - 1)),
        dma((chunks, PARTS)),
        dma((2, chunks, PARTS)),
        dma((chunks, PARTS)),
        dma((chunks, PARTS)),
        dma((chunks,)),
        dma((sums, chunks)),
        dma((sums, chunks)),
        dma((far, far_chunks)),
        dma((sums, chunks)),
        dma((sums, chunks)),
        dma((sums, chunks)),
        dma((sums, chunks)),
        dma((sums, chunks)),
        dma((2, tails, chunks)),
    ]
    dims = (rows_n, cols_n, rhs_n, chain, blocks, chunks, width)
    any_spec = pl.BlockSpec(memory_space=pl.ANY)
    found = pl.pallas_call(
        functools.partial(kernel, dims),
        out_shape=(
            jax.ShapeDtypeStruct((chain, mc, right.shape[2]), f32),
            jax.ShapeDtypeStruct((tails, mr, right.shape[2]), f32),
        ),
        in_specs=[any_spec] * 3,
        out_specs=(any_spec, any_spec),
        scratch_shapes=scratch,
        compiler_params=pltpu.CompilerParams(
            collective_id=0, has_side_effects=True, vmem_limit_bytes=62 * 1024 * 1024
        ),
        cost_estimate=pl.CostEstimate(
            flops=6 * (pairs + chain) * mr * mc * right.shape[2], bytes_accessed=4 * lower.size * 2, transcendentals=0
        ),
    )(lower, inverse, right)
    shapes = tuple(jax.ShapeDtypeStruct(array.shape, array.dtype) for array in found)
    return pl.pallas_call(
        hand_over,
        out_shape=shapes,
        in_specs=[any_spec] * 2,
        out_specs=(any_spec, any_spec),
        scratch_shapes=[
            *(pltpu.VMEM(shape.shape, shape.dtype) for shape in shapes),
            dma((2, chain, 2)),
            dma((2, tails, 2)),
        ],
        compiler_params=pltpu.CompilerParams(vmem_limit_bytes=62 * 1024 * 1024),
        cost_estimate=pl.CostEstimate(
            flops=0, bytes_accessed=8 * sum(array.size for array in found), transcendentals=0
        ),
    )(*found)


def solution(mesh):
    placed = (P(None, "row", None, "col"), P(None, ("col", "rhs"), "row"), P(None, "row", "rhs"))
    return jax.shard_map(
        functools.partial(on_device, mesh),
        mesh=mesh,
        in_specs=placed,
        out_specs=(P(None, "col", "rhs"), P(None, "row", "rhs")),
        check_vma=False,
    )
```

```python
import functools

import jax
import jax.numpy as jnp
from jax import lax
from jax.experimental import pallas as pl
from jax.experimental.pallas import tpu as pltpu
from jax.sharding import PartitionSpec as P

MESH = pl.DeviceIdType.MESH
LANES = 128
PARTS = 4
EARLY = 2


def split(value):
    high = value.astype(jnp.bfloat16)
    return high, (value - high.astype(jnp.float32)).astype(jnp.bfloat16)


def line_role(place, count):
    half = count // 2
    left = place < half
    inward = jnp.where(left, place + 1, place - 1)
    outward = jnp.where(left, place - 1, place + 1)
    from_end = jnp.where(left, place, count - 1 - place)
    return inward, outward, from_end, half - 1 - from_end


def kernel(
    dims, lower, inverse, right, solved, trailing,
    low_hi, low_lo, inv_hi, inv_lo, stage, inv_land, first, acc, zval, zin, zmid, x1, x2, x3, xin, pair, duo,
    stage_sem, first_sem, acc_sem, inv_own_sem, inv_send, inv_recv,
    zin_recv, zmid_recv, z_in_send, z_out_send, sol_sem,
    x1_send, x1_recv, xin_recv, x2_recv, x_in_send, x_out_send, x3_send, x3_recv, tra_sem,
):
    rows_n, cols_n, rhs_n, chain, blocks, chunks, width = dims
    line_n = cols_n // 2
    zhalf, xhalf = rows_n // 2, line_n // 2
    mr, mc = acc.shape[2], zval.shape[1]
    mrh, mch = mr // 2, mc // PARTS
    solved_at = rows_n - 1
    x_at = solved_at + 1
    last_at = x_at + line_n
    spacing = max(chunks, last_at + 1)
    slots = (chain - 1) * spacing + chunks + last_at

    me_row, me_col, me_rhs = lax.axis_index("row"), lax.axis_index("col"), lax.axis_index("rhs")
    core, chip = lax.rem(me_col, 2), lax.div(me_col, 2)
    sibling = me_col + 1 - 2 * core
    z_in, z_out, z_end, z_mid = line_role(me_row, rows_n)
    xc_in, xc_out, x_end, x_mid = line_role(chip, line_n)
    x_in, x_out = xc_in * 2 + core, xc_out * 2 + core
    own = pl.ds(pl.multiple_of(core * mrh, mrh), mrh)
    other = pl.ds(pl.multiple_of((1 - core) * mrh, mrh), mrh)

    barrier = pltpu.get_barrier_semaphore()

    def greet(device):
        pl.semaphore_signal(barrier, inc=1, device_id=device, device_id_type=MESH)

    greet({"row": z_in})
    greet({"col": sibling})
    greet({"col": x_in})
    for step in range(1, rhs_n):
        greet({"rhs": lax.rem(me_rhs + step, rhs_n)})
    if zhalf > 1:
        @pl.when(z_end > 0)
        def _():
            greet({"row": z_out})
    if xhalf > 1:
        @pl.when(x_end > 0)
        def _():
            greet({"col": x_out})
    count = 2 + rhs_n
    if zhalf > 1:
        count += (z_end > 0).astype(jnp.int32)
    if xhalf > 1:
        count += (x_end > 0).astype(jnp.int32)
    pl.semaphore_wait(barrier, count)

    def remote(src, dst, send, recv, device):
        return pltpu.make_async_remote_copy(
            src_ref=src, dst_ref=dst, send_sem=send, recv_sem=recv, device_id=device, device_id_type=MESH
        )

    part = inverse.shape[1]
    mine = pl.ds(pl.multiple_of(me_rhs * part, part), part)

    def inv_copy(k, step):
        return remote(
            inverse.at[k], inv_land.at[k, mine], inv_send.at[k, step - 1], inv_recv.at[k, step - 1],
            {"rhs": lax.rem(me_rhs + step, rhs_n)},
        )

    def inv_own(k):
        return pltpu.make_async_copy(inverse.at[k], inv_land.at[k, mine], inv_own_sem.at[k])

    def inv_start(k):
        for step in range(1, rhs_n):
            inv_copy(k, step).start()
        inv_own(k).start()

    inv_start(0)

    def columns(c):
        return pl.ds(pl.multiple_of(c * width, width), width)

    def first_copy(c):
        return pltpu.make_async_copy(right.at[0, :, columns(c)], first.at[c], first_sem.at[c])

    def acc_copy(j, c):
        return pltpu.make_async_copy(right.at[j + 1, :, columns(c)], acc.at[j, c], acc_sem.at[j, c])

    def each_acc(action):
        @pl.loop(0, (blocks - 1) * chunks)
        def _(n):
            action(lax.div(n, chunks), lax.rem(n, chunks))

    @pl.loop(0, chunks)
    def _(c):
        first_copy(c).start()

    pairs, slot_n = low_hi.shape[0], stage.shape[0]

    def place(k, i):
        return k * (blocks - 1) - lax.div(k * (k - 1), 2) + i - k - 1

    def stage_copy(spot, action):
        for k in range(chain):
            begin = k * (blocks - 1) - (k * (k - 1)) // 2
            end = begin + blocks - 1 - k

            @pl.when((spot >= begin) & (spot < end))
            def _():
                at = lax.rem(spot, slot_n)
                action(pltpu.make_async_copy(lower.at[spot - begin + k + 1, :, k, :], stage.at[at], stage_sem.at[at]))

    def take_block(spot):
        @pl.when((spot >= 0) & (spot < pairs))
        def _():
            stage_copy(spot, lambda copy: copy.wait())
            low_hi[spot], low_lo[spot] = split(stage[lax.rem(spot, slot_n)])

            @pl.when(spot + slot_n < pairs)
            def _():
                stage_copy(spot + slot_n, lambda copy: copy.start())

    @pl.loop(0, min(slot_n, pairs))
    def _(spot):
        stage_copy(spot, lambda copy: copy.start())

    @pl.loop(0, chunks)
    def _(c):
        first_copy(c).wait()

    def product(high, low, depth):
        both = jnp.dot(high, pair[:depth, :], preferred_element_type=jnp.float32)
        rest = jnp.dot(low, pair[:depth, :width], preferred_element_type=jnp.float32)
        return both[:, :width] + (both[:, width:] + rest)

    def set_pair(rows, value):
        high, low = split(value)
        pair[rows, :width] = high
        pair[rows, width:] = low

    own_parts = PARTS // rhs_n

    def z_rows(h):
        at = lax.rem(h + me_rhs * own_parts, PARTS)
        return pl.ds(pl.multiple_of(at * mch, mch), mch)

    def z_to_middle(k, c, h):
        return remote(zval.at[c, z_rows(h)], zmid.at[lax.rem(k, 2), c, z_rows(h)], z_in_send.at[c, h],
                      zmid_recv.at[lax.rem(k, 2), c, h], {"row": z_in})

    def z_inward(c, h):
        return remote(zval.at[c, z_rows(h)], zin.at[c, z_rows(h)], z_in_send.at[c, h], zin_recv.at[c, h], {"row": z_in})

    def z_outward(k, c, h):
        at = zmid.at[lax.rem(k, 2), c, z_rows(h)]
        return remote(at, at, z_out_send.at[c, h], zmid_recv.at[lax.rem(k, 2), c, h], {"row": z_out})

    def tail(j):
        return jnp.maximum(j - (chain - 1), 0)

    def x_first(j, c):
        return remote(acc.at[j, c, other], x1.at[tail(j), c], x1_send.at[j, c], x1_recv.at[j, c], {"col": sibling})

    def x_to_middle(j, c):
        return remote(acc.at[j, c, own], x2.at[j, c], x_in_send.at[j, c], x2_recv.at[j, c], {"col": x_in})

    def x_inward(j, c):
        return remote(acc.at[j, c, own], xin.at[j, c], x_in_send.at[j, c], xin_recv.at[j, c], {"col": x_in})

    def x_outward(j, c):
        return remote(x2.at[j, c], x2.at[j, c], x_out_send.at[j, c], x2_recv.at[j, c], {"col": x_out})

    def x_back(j, c):
        return remote(x2.at[j, c], x3.at[tail(j), c], x3_send.at[j, c], x3_recv.at[j, c], {"col": sibling})

    def solved_copy(k, c):
        return pltpu.make_async_copy(zmid.at[lax.rem(k, 2), c], solved.at[k, :, columns(c)], sol_sem.at[c])

    def trailing_own(j, c):
        return pltpu.make_async_copy(
            x2.at[j, c], trailing.at[j - (chain - 1), own, columns(c)], tra_sem.at[0, j - (chain - 1), c])

    def trailing_other(j, c):
        return pltpu.make_async_copy(
            x3.at[tail(j), c], trailing.at[j - (chain - 1), other, columns(c)], tra_sem.at[1, j - (chain - 1), c])

    def item(t, lag, then):
        u = t - lag
        n = jnp.maximum(u, 0)
        k, c = lax.div(n, spacing), lax.rem(n, spacing)

        @pl.when((u >= 0) & (k < chain) & (c < chunks))
        def _():
            then(k, c)

    def each_sum(k, action):
        stop = jnp.where(k == chain - 1, blocks - 1, k + 1)

        @pl.loop(k, stop)
        def _(j):
            action(j)

    def z_steps(h):
        def inward_part(k, c):
            if zhalf > 1:
                @pl.when(z_end > 0)
                def _():
                    z_inward(c, h).wait_recv()
                    zval[c, z_rows(h)] += zin[c, z_rows(h)]

                @pl.when(z_mid > 0)
                def _():
                    z_inward(c, h).start()

            @pl.when(z_mid == 0)
            def _():
                z_to_middle(k, c, h).start()

        def outward_part(k, c):
            z_to_middle(k, c, h).wait_recv()

            @pl.when(z_mid == 0)
            def _():
                zmid[lax.rem(k, 2), c, z_rows(h)] += zval[c, z_rows(h)]

            if zhalf > 1:
                @pl.when(z_end > 0)
                def _():
                    z_outward(k, c, h).start()

        return inward_part, outward_part

    def z_part(t, h):
        for lag, step in zip((z_end, zhalf + z_mid), z_steps(h)):
            def once(k, c, step=step):
                if h >= own_parts:
                    step(k, c)
                else:
                    @pl.when((k > 0) | (c >= EARLY))
                    def _():
                        step(k, c)

            item(t, lag, once)

    def x_part(t):
        def inward_part(k, c):
            def one(j):
                x_first(j, c).wait_recv()
                acc[j, c, own] += x1[tail(j), c]
                if xhalf > 1:
                    @pl.when(x_end > 0)
                    def _():
                        x_inward(j, c).wait_recv()
                        acc[j, c, own] += xin[j, c]

                    @pl.when(x_mid > 0)
                    def _():
                        x_inward(j, c).start()

                @pl.when(x_mid == 0)
                def _():
                    x_to_middle(j, c).start()

            each_sum(k, one)

        def outward_part(k, c):
            def one(j):
                x_to_middle(j, c).wait_recv()

                @pl.when(x_mid == 0)
                def _():
                    x2[j, c] += acc[j, c, own]

                x_back(j, c).start()
                if xhalf > 1:
                    @pl.when(x_end > 0)
                    def _():
                        x_outward(j, c).start()

            each_sum(k, one)

        def last_part(k, c):
            def one(j):
                x_back(j, c).wait_recv()
                x_first(j, c).wait_send()
                x_to_middle(j, c).wait_send()
                x_back(j, c).wait_send()
                if xhalf > 1:
                    @pl.when(x_end > 0)
                    def _():
                        x_outward(j, c).wait_send()

                @pl.when(k == chain - 1)
                def _():
                    trailing_own(j, c).start()
                    trailing_other(j, c).start()

            each_sum(k, one)

        item(t, x_at + x_end, inward_part)
        item(t, x_at + xhalf + x_mid, outward_part)
        item(t, last_at, last_part)

    def value_part(k, c):
        @pl.when(c == 0)
        def _():
            for step in range(1, rhs_n):
                inv_copy(k, step).wait()

            @pl.when(k > 0)
            def _():
                inv_own(k).wait()

            @pl.when(k + 1 < chain)
            def _():
                inv_start(k + 1)

            inv_hi[k], inv_lo[k] = split(inv_land[k])

        @pl.when(k == 0)
        def _():
            set_pair(pl.ds(0, mr), first[c])

        @pl.when(k > 0)
        def _():
            before = jnp.maximum(k - 1, 0)
            set_pair(own, x2[before, c])
            set_pair(other, x3[0, c])

        @pl.when((k > 0) | (c >= EARLY))
        def _():
            zval[c] = product(inv_hi[k], inv_lo[k], mr)

        @pl.when((k == 0) & (c < EARLY))
        def _():
            for step in range(1, rhs_n):
                value_rows(0, c, lax.rem(me_rhs + step, rhs_n))

    def value_rows(k, c, group):
        rows = pl.ds(pl.multiple_of(group * part, part), part)
        zval[c, rows] = product(inv_hi[k, rows], inv_lo[k, rows], mr)

    def update_part(k, c):
        solved_copy(k, c).start()
        for h in range(PARTS):
            z_inward(c, h).wait_send()
        set_pair(pl.ds(0, mc), zmid[lax.rem(k, 2), c])

        @pl.loop(k + 1, jnp.where(k == chain - 1, blocks, k + 2))
        def _(i):
            spot = place(k, i)
            acc[i - 1, c] -= product(low_hi[spot], low_lo[spot], mc)
            x_first(i - 1, c).start()

    def far_part(k, c):
        @pl.when(k < chain - 1)
        def _():
            for odd in range(2):
                @pl.when(lax.rem(c, 2) == odd)
                def _():
                    duo[:, odd * width:(odd + 1) * width] = pair[:mc, :width]
                    duo[:, (odd + 2) * width:(odd + 3) * width] = pair[:mc, width:]

            @pl.when(lax.rem(c, 2) == 1)
            def _():
                update_two(k, c, k + 2, jnp.minimum(k + 4, blocks))

    def update_two(k, c, begin, end):
        before = jnp.maximum(c - 1, 0)

        @pl.loop(begin, end)
        def _(i):
            spot = place(k, i)
            wide = jnp.dot(low_hi[spot], duo[...], preferred_element_type=jnp.float32)
            rest = jnp.dot(low_lo[spot], duo[:, :2 * width], preferred_element_type=jnp.float32)
            both = wide[:, :2 * width] + (wide[:, 2 * width:] + rest)
            acc[i - 1, before] -= both[:, :width]
            acc[i - 1, c] -= both[:, width:]

    def rest_part(k, c):
        @pl.when((k < chain - 1) & (lax.rem(c, 2) == 1))
        def _():
            update_two(k, c, k + 4, jnp.maximum(blocks, k + 4))

    def release_part(k, c):
        solved_copy(k, c).wait()
        if zhalf > 1:
            @pl.when(z_end > 0)
            def _():
                for h in range(PARTS):
                    z_outward(k, c, h).wait_send()

    inv_own(0).wait()
    inv_hi[0, mine], inv_lo[0, mine] = split(inv_land[0, mine])
    for c in range(EARLY):
        set_pair(pl.ds(0, mr), first[c])
        value_rows(0, c, me_rhs)
        for h in range(own_parts):
            z_steps(h)[0](0, c)
    @pl.when(me_col == 0)
    def _():
        each_acc(lambda j, c: acc_copy(j, c).start())

    @pl.when(me_col != 0)
    def _():
        def clear(j, c):
            acc[j, c] = jnp.zeros((mr, width), jnp.float32)

        each_acc(clear)

    taken = min(2, pairs)
    for spot in range(taken):
        take_block(spot)
    for c in range(EARLY):
        for h in range(own_parts):
            z_steps(h)[1](0, c)

    @pl.loop(0, slots + 1)
    def _(n):
        t = n - 1
        for h in range(PARTS // 2):
            z_part(t, h)
        x_part(t)
        item(t, -1, value_part)
        item(t, solved_at + 1, rest_part)
        for h in range(PARTS // 2, PARTS):
            z_part(t, h)
        item(t, solved_at + 1, release_part)

        @pl.when((t == 0) & (me_col == 0))
        def _():
            each_acc(lambda j, c: acc_copy(j, c).wait())

        item(t, solved_at, update_part)
        item(t, solved_at, far_part)
        take_block(jnp.where(t + 1 >= taken, t + 1, -1))

    @pl.loop(0, (blocks - chain) * chunks)
    def _(n):
        j, c = chain - 1 + lax.div(n, chunks), lax.rem(n, chunks)
        trailing_own(j, c).wait()
        trailing_other(j, c).wait()


def hand_over(solved, trailing, solved_out, trailing_out, solved_buf, trailing_buf, solved_sem, trailing_sem):
    jobs = []
    for src, buf, dst, sems in (
        (solved, solved_buf, solved_out, solved_sem), (trailing, trailing_buf, trailing_out, trailing_sem),
    ):
        rows = src.shape[1] // 2
        for k in range(src.shape[0]):
            for half in range(2):
                at = pl.ds(half * rows, rows)
                jobs.append((
                    pltpu.make_async_copy(src.at[k, at], buf.at[k, at], sems.at[0, k, half]),
                    pltpu.make_async_copy(buf.at[k, at], dst.at[k, at], sems.at[1, k, half]),
                ))
    for come, _ in jobs:
        come.start()
    for come, go in jobs:
        come.wait()
        go.start()
    for _, go in jobs:
        go.wait()


def on_device(mesh, lower, inverse, right):
    rows_n, cols_n, rhs_n = mesh.shape["row"], mesh.shape["col"], mesh.shape["rhs"]
    blocks, mr, chain, mc = lower.shape
    width = LANES
    chunks = right.shape[2] // width
    assert chunks % 2 == 0
    part = inverse.shape[1]
    pairs = sum(blocks - 1 - k for k in range(chain))
    sums = blocks - 1
    stages = min(4, pairs)
    tails = blocks - chain
    mrh = mr // 2
    f32, bf16 = jnp.float32, jnp.bfloat16
    far = sums if cols_n > 4 else 1
    far_chunks = chunks if cols_n > 4 else 1
    dma = pltpu.SemaphoreType.DMA
    scratch = [
        pltpu.VMEM((pairs, mr, mc), bf16),
        pltpu.VMEM((pairs, mr, mc), bf16),
        pltpu.VMEM((chain, mc, mr), bf16),
        pltpu.VMEM((chain, mc, mr), bf16),
        pltpu.VMEM((stages, mr, mc), f32),
        pltpu.VMEM((chain, mc, mr), f32),
        pltpu.VMEM((chunks, mr, width), f32),
        pltpu.VMEM((sums, chunks, mr, width), f32),
        pltpu.VMEM((chunks, mc, width), f32),
        pltpu.VMEM((chunks, mc, width), f32),
        pltpu.VMEM((2, chunks, mc, width), f32),
        pltpu.VMEM((tails, chunks, mrh, width), f32),
        pltpu.VMEM((sums, chunks, mrh, width), f32),
        pltpu.VMEM((tails, chunks, mrh, width), f32),
        pltpu.VMEM((far, far_chunks, mrh, width), f32),
        pltpu.VMEM((max(mr, mc), 2 * width), bf16),
        pltpu.VMEM((mc, 4 * width), bf16),
        dma((stages,)),
        dma((chunks,)),
        dma((sums, chunks)),
        dma((chain,)),
        dma((chain, rhs_n - 1)),
        dma((chain, rhs_n - 1)),
        dma((chunks, PARTS)),
        dma((2, chunks, PARTS)),
        dma((chunks, PARTS)),
        dma((chunks, PARTS)),
        dma((chunks,)),
        dma((sums, chunks)),
        dma((sums, chunks)),
        dma((far, far_chunks)),
        dma((sums, chunks)),
        dma((sums, chunks)),
        dma((sums, chunks)),
        dma((sums, chunks)),
        dma((sums, chunks)),
        dma((2, tails, chunks)),
    ]
    dims = (rows_n, cols_n, rhs_n, chain, blocks, chunks, width)
    any_spec = pl.BlockSpec(memory_space=pl.ANY)
    found = pl.pallas_call(
        functools.partial(kernel, dims),
        out_shape=(
            jax.ShapeDtypeStruct((chain, mc, right.shape[2]), f32),
            jax.ShapeDtypeStruct((tails, mr, right.shape[2]), f32),
        ),
        in_specs=[any_spec] * 3,
        out_specs=(any_spec, any_spec),
        scratch_shapes=scratch,
        compiler_params=pltpu.CompilerParams(
            collective_id=0, has_side_effects=True, vmem_limit_bytes=62 * 1024 * 1024
        ),
        cost_estimate=pl.CostEstimate(
            flops=6 * (pairs + chain) * mr * mc * right.shape[2], bytes_accessed=4 * lower.size * 2, transcendentals=0
        ),
    )(lower, inverse, right)
    shapes = tuple(jax.ShapeDtypeStruct(array.shape, array.dtype) for array in found)
    return pl.pallas_call(
        hand_over,
        out_shape=shapes,
        in_specs=[any_spec] * 2,
        out_specs=(any_spec, any_spec),
        scratch_shapes=[
            *(pltpu.VMEM(shape.shape, shape.dtype) for shape in shapes),
            dma((2, chain, 2)),
            dma((2, tails, 2)),
        ],
        compiler_params=pltpu.CompilerParams(vmem_limit_bytes=62 * 1024 * 1024),
        cost_estimate=pl.CostEstimate(
            flops=0, bytes_accessed=8 * sum(array.size for array in found), transcendentals=0
        ),
    )(*found)


def solution(mesh):
    placed = (P(None, "row", None, "col"), P(None, ("col", "rhs"), "row"), P(None, "row", "rhs"))
    return jax.shard_map(
        functools.partial(on_device, mesh),
        mesh=mesh,
        in_specs=placed,
        out_specs=(P(None, "col", "rhs"), P(None, "row", "rhs")),
        check_vma=False,
    )
```
